32 devices in a mesh: req: 16 (over z, x, core), tp: 2 (over y).
Axes of the slice: x: 2, y: 2, z: 4, core: 2. Of those that a mesh axis runs over, the one named last changes fastest.
Arguments:
- query_new: bfloat16 [64, 2048], P('req', 'tp'), may hold values from -16 to 16
- key_new: bfloat16 [64, 2048], P('req', 'tp'), may hold values from -6 to 6
- value_new: bfloat16 [64, 2048], P('req', 'tp'), may hold values from -6 to 6
- residual: bfloat16 [64, 2048], P('req', 'tp'), may hold values from -3 to 3
- dense_weight: bfloat16 [2048, 2048], P('tp'), may hold values from -1 to 1
- dense_bias: bfloat16 [2048], P('tp'), may hold values from -3 to 3
- key_pool: bfloat16 [384, 128, 2048], P('req', None, 'tp'), may hold values from -8 to 8
- value_pool: bfloat16 [384, 128, 2048], P('req', None, 'tp'), may hold values from -6 to 6
- page_table: int32 [64, 8], P('req'), may hold values from 0 to 23, as said below
- lengths: int32 [64], P('req'), may hold values from 0 to 1023, as said below
- request_slot: int32 [64], P('req'), may hold values from 0 to 63, as said below
- arrival_index: int32 [64], P('req'), may hold values from 0 to 63, as said below
Outputs:
- hidden: bfloat16 [64, 2048], P('req', 'tp')
- appended_keys: bfloat16 [64, 2048], P('req', 'tp')
- appended_values: bfloat16 [64, 2048], P('req', 'tp')
The draws below stay inside these ranges and needn't reach their ends.
Inputs may be any that keep to these rules, and one draw needn't show every extreme that they name: All entries differ; request_slot[r] is the resident slot of arrival request r, and slot s lies on req device s // 4. arrival_index[s] = r exactly where request_slot[r] = s. `page_table`: the first 2 * ceil((lengths[s] + 1) / 256) entries of a row name pages of its own req device's pool, all different from each other and from those of the other slots of that device; later entries name arbitrary pages of that pool and are not read. The pages that the slots of one req device need, 2 * ceil((lengths[s] + 1) / 256) each, number at most 24 in all.
All inputs are finite; a program needn't handle non-finite values.
Results may differ from the reference program's by a relative error of at most 0.011.
Values may be sent and summed in bfloat16 or wider, within the bound.
No kernel may reach another device: no remote copies, remote signals or barrier semaphores. Data moves between devices by JAX's collectives and lax.ppermute only.
A program may use at most 64 MiB of HBM per device.

```python
import jax
import jax.numpy as jnp
from jax import lax

D = 2048
HEADS = 8
HS = 256
PAGE = 128
MAXP = 8
R_DEV = 4
REQS = 64
POOL_DEV = 24
POOL = 384


def draw_query_new(key, part):
    base = jnp.clip(jax.random.normal(jax.random.fold_in(key, 1), (REQS, HEADS, HS), jnp.float32), -6.0, 6.0)
    return base.reshape(REQS, HEADS * HS).astype(jnp.bfloat16)


def draw_key_pool(key, part):
    base = jnp.clip(jax.random.normal(jax.random.fold_in(key, 4), (POOL, PAGE, HEADS, HS), jnp.float32), -6.0, 6.0)
    return base.reshape(POOL, PAGE, HEADS * HS).astype(jnp.bfloat16)


def page_plan(key):
    devices = REQS // R_DEV
    most_units = (MAXP - 2) // 2
    cap_units = R_DEV * MAXP // 4
    raw = jax.random.randint(jax.random.fold_in(key, 21), (devices, R_DEV), 0, most_units + 1)
    busy = jax.random.randint(jax.random.fold_in(key, 26), (devices, 1), 0, 2)
    raw = raw * busy
    before = jnp.cumsum(raw, axis=1) - raw
    units = jnp.minimum(raw, jnp.maximum(cap_units - before, 0))
    greedy = jnp.clip(cap_units - most_units * jnp.arange(R_DEV), 0, most_units)
    greedy = greedy[jax.random.permutation(jax.random.fold_in(key, 22), R_DEV)]
    full_device = jax.random.randint(jax.random.fold_in(key, 23), (), 0, devices)
    is_full = (jnp.arange(devices) == full_device)[:, None]
    units = jnp.where(is_full, greedy[None, :], units)
    counts = 2 + 2 * units
    offset = jax.random.randint(jax.random.fold_in(key, 24), (devices, R_DEV), 0, 2 * PAGE)
    lengths = (counts - 2) * PAGE + offset
    lengths = jnp.where(is_full & (units == most_units), counts * PAGE - 1, lengths)
    pool_order = jax.vmap(lambda sub: jax.random.permutation(sub, POOL_DEV))(jax.random.split(jax.random.fold_in(key, 25), devices))
    start = jnp.cumsum(counts, axis=1) - counts
    position = (start[:, :, None] + jnp.arange(MAXP)[None, None, :]) % POOL_DEV
    table = jnp.take_along_axis(jnp.broadcast_to(pool_order[:, None, :], (devices, R_DEV, POOL_DEV)), position, axis=2)
    return (table.reshape(REQS, MAXP).astype(jnp.int32), lengths.reshape(REQS).astype(jnp.int32))


def draw_page_table(key, part):
    return page_plan(key)[0]


def draw_lengths(key, part):
    return page_plan(key)[1]


def slot_plan(key):
    slots = jax.random.permutation(jax.random.fold_in(key, 31), REQS).astype(jnp.int32)
    inverse = jnp.argsort(slots).astype(jnp.int32)
    return (slots, inverse)


def draw_request_slot(key, part):
    return slot_plan(key)[0]


def draw_arrival_index(key, part):
    return slot_plan(key)[1]


def levels(key, dims, pieces, least, largest):
    def one(axis_at, blocks):
        steps = jax.random.uniform(jax.random.fold_in(jax.random.fold_in(key, 6), axis_at), (blocks,), jnp.float32, least / len(pieces), largest / len(pieces))
        return jnp.repeat(jnp.exp(steps), dims[axis_at] // blocks).reshape((-1,) + (1,) * (len(dims) - axis_at - 1))

    loudness = one(*pieces[0])
    for cut in pieces[1:]:
        loudness = loudness * one(*cut)
    return loudness


def gaussian(key, dims, deviation, most, shards=(), kind=jnp.bfloat16):
    loudness = levels(key, dims, shards, -0.22, 0.18) if shards else 1.0
    drawn = jax.random.normal(key, dims, jnp.float32) * deviation * loudness
    return jnp.minimum(jnp.maximum(drawn, -most), most).astype(kind)


def setup_inputs(seed: int = 0) -> dict:
    streams_of = jax.random.split(jax.random.key(seed), 13)
    return {
        "query_new": draw_query_new(jax.random.fold_in(streams_of[12], 71), 0),
        "key_new": gaussian(streams_of[1], (REQS, HEADS * HS), 1.0, 6.0, ((0, 16), (1, 2))),
        "value_new": gaussian(streams_of[2], (REQS, HEADS * HS), 1.0, 6.0, ((0, 16), (1, 2))),
        "residual": gaussian(streams_of[3], (REQS, D), 0.5, 3.0, ((0, 16), (1, 2))),
        "dense_weight": gaussian(streams_of[4], (HEADS * HS, D), (HEADS * HS // 64) ** -0.5, 1.0, ((0, 2),)),
        "dense_bias": gaussian(streams_of[5], (D,), 0.5, 3.0, ((0, 2),)),
        "key_pool": draw_key_pool(jax.random.fold_in(streams_of[12], 71), 0),
        "value_pool": gaussian(streams_of[7], (POOL, PAGE, HEADS * HS), 1.0, 6.0, ((0, 16), (2, 2))),
        "page_table": draw_page_table(jax.random.fold_in(streams_of[12], 71), 0),
        "lengths": draw_lengths(jax.random.fold_in(streams_of[12], 71), 0),
        "request_slot": draw_request_slot(jax.random.fold_in(streams_of[12], 71), 0),
        "arrival_index": draw_arrival_index(jax.random.fold_in(streams_of[12], 71), 0),
    }


def rotate(vectors, positions):
    head_size = vectors.shape[-1]
    rotary_dims = head_size // 4
    half_dims = rotary_dims // 2
    rates = 10000.0 ** (-2.0 * jnp.arange(half_dims, dtype=jnp.float32) / rotary_dims)
    angle = positions.astype(jnp.float32)[:, None] * rates[None, :]
    cosine = jnp.cos(angle)[:, None, :]
    sine = jnp.sin(angle)[:, None, :]
    front_half = vectors[..., :half_dims]
    back_half = vectors[..., half_dims:rotary_dims]
    return jnp.concatenate([front_half * cosine - back_half * sine, back_half * cosine + front_half * sine, vectors[..., rotary_dims:]], axis=-1)


def reference(query_new, key_new, value_new, residual, dense_weight, dense_bias, key_pool, value_pool, page_table, lengths, request_slot, arrival_index):
    scale = HS ** -0.5
    query = query_new[arrival_index]
    own_key = key_new[arrival_index]
    appended_values = value_new[arrival_index]
    rotated_query = rotate(query.astype(jnp.float32).reshape(REQS, HEADS, HS), lengths).astype(jnp.bfloat16)
    appended_keys = rotate(own_key.astype(jnp.float32).reshape(REQS, HEADS, HS), lengths).astype(jnp.bfloat16)
    value_heads = appended_values.reshape(REQS, HEADS, HS)
    owner_offset = (jnp.arange(REQS, dtype=jnp.int32) // R_DEV) * POOL_DEV
    global_pages = (page_table + owner_offset[:, None]).astype(jnp.int32)

    def one_request(items):
        query_one, key_one, value_one, pages, length = items
        key_pages = key_pool[pages].astype(jnp.float32).reshape(MAXP * PAGE, HEADS, HS)
        value_pages = value_pool[pages].astype(jnp.float32).reshape(MAXP * PAGE, HEADS, HS)
        scores = jnp.einsum('hd,thd->ht', query_one.astype(jnp.float32), key_pages) * scale
        own_score = jnp.sum(query_one.astype(jnp.float32) * key_one.astype(jnp.float32), axis=-1) * scale
        visible = jnp.arange(MAXP * PAGE, dtype=jnp.int32) < length
        masked = jnp.where(visible[None, :], scores, -jnp.inf)
        top = jnp.maximum(jnp.max(masked, axis=1), own_score)
        spread = jnp.exp(masked - top[:, None])
        own_spread = jnp.exp(own_score - top)
        total = jnp.sum(spread, axis=1) + own_spread
        weights = (spread / total[:, None]).astype(jnp.bfloat16)
        own_weight = (own_spread / total).astype(jnp.bfloat16)
        attended = jnp.einsum('ht,thd->hd', weights.astype(jnp.float32), value_pages)
        attended = attended + own_weight.astype(jnp.float32)[:, None] * value_one.astype(jnp.float32)
        return attended.astype(jnp.bfloat16).reshape(HEADS * HS)

    attended = lax.map(one_request, (rotated_query, appended_keys, value_heads, global_pages, lengths))
    projected = jnp.dot(attended, dense_weight, preferred_element_type=jnp.float32).astype(jnp.bfloat16)
    back = projected[request_slot]
    hidden = (residual.astype(jnp.float32) + dense_bias.astype(jnp.float32)[None, :] + back.astype(jnp.float32)).astype(jnp.bfloat16)
    return hidden, appended_keys.reshape(REQS, HEADS * HS), appended_values
```

```python
import functools

import jax
import jax.numpy as jnp
from jax import lax
from jax.experimental import pallas as pl
from jax.experimental.pallas import tpu as pltpu
from jax.sharding import PartitionSpec as P

HS = 256
BF16 = jnp.bfloat16
F32 = jnp.float32
ANY = pl.BlockSpec(memory_space=pl.ANY)
VMEM = pl.BlockSpec(memory_space=pltpu.VMEM)
SMEM = pl.BlockSpec(memory_space=pltpu.SMEM)


def gather_by_doubling(block, devices):
    held = block[None]
    bit = devices // 2
    while bit:
        pairs = [(i, i ^ bit) for i in range(devices)]
        held = jnp.concatenate([held, lax.ppermute(held, "req", pairs)], axis=0)
        bit //= 2
    return held


def place_of(owner, me, devices):
    apart = owner ^ me
    place = jnp.int32(0)
    bit, weight = devices // 2, 1
    while bit:
        place = place + jnp.where((apart & bit) != 0, weight, 0)
        bit //= 2
        weight *= 2
    return place


def sum_by_halving(kept, sent, parts):
    bit = parts // 2
    while True:
        kept = kept + lax.ppermute(sent, "tp", [(i, i ^ bit) for i in range(parts)])
        if bit == 1:
            return kept[0]
        bit //= 2
        kept, sent = kept[:bit], kept[bit:]


def take_row(block, row):
    block = block.astype(F32)
    rows = lax.broadcasted_iota(jnp.int32, block.shape, 0)
    return jnp.sum(jnp.where(rows == row, block, 0.0), axis=0, keepdims=True)


def rotary_factors(lengths, heads):
    rotary_dims = HS // 4
    half = rotary_dims // 2
    rates = 10000.0 ** (-2.0 * jnp.arange(half, dtype=F32) / rotary_dims)
    angle = lengths.astype(F32)[:, None] * rates[None, :]
    cosine, sine = jnp.cos(angle), jnp.sin(angle)
    rows = lengths.shape[0]
    none = jnp.zeros((rows, half), F32)
    rest = jnp.zeros((rows, HS - rotary_dims), F32)
    same = jnp.concatenate([cosine, cosine, rest + 1.0], axis=1)
    right = jnp.concatenate([-sine, none, rest], axis=1)
    left = jnp.concatenate([none, sine, rest], axis=1)
    return jnp.stack([jnp.tile(f, (1, heads)) for f in (same, right, left)])


def attend(devices, parts, me_ref, arrival_ref, fresh_ref, factors_ref, table_ref, lengths_ref,
           keys_ref, values_ref, weight_ref, kept_out, sent_out, keys_out, values_out, terms_ref):
    me, half = me_ref[0], me_ref[1]
    slots = table_ref.shape[0]
    width = keys_out.shape[1]
    heads = width // HS
    per = fresh_ref.shape[1]
    pages, page = keys_ref.shape[0], keys_ref.shape[1]
    tokens = pages * page
    scale = HS ** (-0.5)

    taken = []
    for s in range(slots):
        arrival = arrival_ref[s]
        block = fresh_ref[place_of(arrival // per, me, devices)]
        taken.append(take_row(block, arrival % per))
    taken = jnp.concatenate(taken, axis=0)
    query, key, value = (taken[:, i * width:(i + 1) * width] for i in range(3))

    def rotate(x):
        right = pltpu.roll(x, width - HS // 8, 1)
        left = pltpu.roll(x, HS // 8, 1)
        return x * factors_ref[0] + right * factors_ref[1] + left * factors_ref[2]

    query = rotate(query).astype(BF16).astype(F32)
    key = rotate(key).astype(BF16)
    keys_out[...] = key
    values_out[...] = value.astype(BF16)

    rows = heads * slots
    row_head = lax.broadcasted_iota(jnp.int32, (rows, width), 0) // slots
    lane_head = lax.broadcasted_iota(jnp.int32, (rows, width), 1) // HS
    mine = row_head == lane_head
    spread_query = jnp.where(mine, jnp.concatenate([query] * heads, axis=0), 0.0)
    own_score = jnp.sum(
        spread_query * jnp.concatenate([key.astype(F32)] * heads, axis=0), axis=1, keepdims=True
    ) * scale

    lane = lax.broadcasted_iota(jnp.int32, (slots, 128), 1)
    visible = jnp.zeros((slots, 128), jnp.int32)
    for i in range(table_ref.shape[1]):
        left_over = jnp.clip(lengths_ref[...] - i * page, 0, page)
        visible = jnp.where((lane == table_ref[:, i:i + 1]) & (left_over > 0), left_over, visible)
    visible = jnp.concatenate([visible] * heads, axis=0)

    scores = lax.dot_general(
        spread_query.astype(BF16), keys_ref[...].reshape(tokens, width),
        (((1,), (1,)), ((), ())), preferred_element_type=F32,
    ) * scale
    place = lax.broadcasted_iota(jnp.int32, (rows, page), 1)
    masked = jnp.concatenate(
        [
            jnp.where(place < visible[:, p:p + 1], scores[:, p * page:(p + 1) * page], -jnp.inf)
            for p in range(pages)
        ],
        axis=1,
    )
    top = jnp.maximum(jnp.max(masked, axis=1, keepdims=True), own_score)
    exps = jnp.exp(masked - top)
    own_exp = jnp.exp(own_score - top)
    total = jnp.sum(exps, axis=1, keepdims=True) + own_exp
    weights = (exps / total).astype(BF16)
    own_weight = (own_exp / total).astype(BF16).astype(F32)
    attended = jnp.dot(weights, values_ref[...].reshape(tokens, width), preferred_element_type=F32)
    attended = attended + own_weight * jnp.concatenate([value] * heads, axis=0)
    attended = jnp.where(mine, attended, 0.0)
    attended = sum(attended[h * slots:(h + 1) * slots] for h in range(heads)).astype(BF16)

    terms = jnp.dot(attended, weight_ref[...], preferred_element_type=F32)
    for part in range(parts):
        terms_ref[part ^ half] = terms[:, part * width:(part + 1) * width]
    kept_out[...] = terms_ref[:parts // 2]
    sent_out[...] = terms_ref[parts // 2:]


def finish(devices, me_ref, slot_ref, held_ref, residual_ref, bias_ref, out_ref):
    me = me_ref[0]
    per = held_ref.shape[1]
    taken = []
    for r in range(out_ref.shape[0]):
        slot = slot_ref[r]
        taken.append(take_row(held_ref[place_of(slot // per, me, devices)], slot % per))
    taken = jnp.concatenate(taken, axis=0)
    out_ref[...] = (residual_ref[...].astype(F32) + bias_ref[...].astype(F32) + taken).astype(BF16)


def on_device(devices, parts, query_new, key_new, value_new, residual, dense_weight, dense_bias,
              key_pool, value_pool, page_table, lengths, request_slot, arrival_index):
    rows, width = query_new.shape
    heads = width // HS
    me = jnp.stack([lax.axis_index("req"), lax.axis_index("tp")]).astype(jnp.int32)
    fresh = gather_by_doubling(jnp.concatenate([query_new, key_new, value_new], axis=1), devices)
    factors = rotary_factors(lengths, heads)
    half_terms = jax.ShapeDtypeStruct((parts // 2, rows, width), F32)
    kept, sent, appended_keys, appended_values = pl.pallas_call(
        functools.partial(attend, devices, parts),
        out_shape=(
            half_terms,
            half_terms,
            jax.ShapeDtypeStruct((rows, width), BF16),
            jax.ShapeDtypeStruct((rows, width), BF16),
        ),
        scratch_shapes=[pltpu.VMEM((parts, rows, width), F32)],
        in_specs=[SMEM, SMEM, VMEM, VMEM, VMEM, VMEM, VMEM, VMEM, VMEM],
        out_specs=(VMEM,) * 4,
        compiler_params=pltpu.CompilerParams(vmem_limit_bytes=32 * 1024 * 1024),
    )(me, arrival_index, fresh, factors, page_table, lengths[:, None], key_pool, value_pool, dense_weight)
    held = gather_by_doubling(sum_by_halving(kept, sent, parts).astype(BF16), devices)
    hidden = pl.pallas_call(
        functools.partial(finish, devices),
        out_shape=jax.ShapeDtypeStruct((rows, width), BF16),
        in_specs=[SMEM, SMEM, VMEM, VMEM, VMEM],
        out_specs=VMEM,
    )(me, request_slot, held, residual, dense_bias[None, :])
    return hidden, appended_keys, appended_values


def solution(mesh):
    rows = P("req", "tp")
    pool = P("req", None, "tp")
    in_specs = (rows,) * 4 + (P("tp", None), P("tp"), pool, pool, P("req", None)) + (P("req"),) * 3
    step = functools.partial(on_device, mesh.shape["req"], mesh.shape["tp"])
    return jax.shard_map(step, mesh=mesh, in_specs=in_specs, out_specs=(rows,) * 3, check_vma=False)
```

```python
import functools

import jax
import jax.numpy as jnp
from jax import lax
from jax.experimental import pallas as pl
from jax.experimental.pallas import tpu as pltpu
from jax.sharding import PartitionSpec as P

HS = 256
BF16 = jnp.bfloat16
F32 = jnp.float32
ANY = pl.BlockSpec(memory_space=pl.ANY)
VMEM = pl.BlockSpec(memory_space=pltpu.VMEM)


def joined(own_ref, other_ref, out_ref):
    count = own_ref.shape[0]
    out_ref[:count] = own_ref[...]
    out_ref[count:] = other_ref[...]


def join(own, other, work):
    return pl.pallas_call(
        joined,
        out_shape=jax.ShapeDtypeStruct((2 * own.shape[0],) + own.shape[1:], own.dtype),
        in_specs=[VMEM, VMEM],
        out_specs=VMEM,
        cost_estimate=pl.CostEstimate(flops=work, bytes_accessed=work >> 14, transcendentals=0),
        compiler_params=pltpu.CompilerParams(vmem_limit_bytes=1 << 20),
    )(own, other)


def gather_by_doubling(block, devices, works):
    held = block[None]
    bit = devices // 2
    while True:
        other = lax.ppermute(held, "req", [(i, i ^ bit) for i in range(devices)])
        if bit == 1:
            return held, other
        held = join(held, other, works.pop(0) if works else 0)
        bit //= 2


def places(rows, per, devices):
    apart = (rows // per) ^ lax.axis_index("req").astype(jnp.int32)
    place = jnp.zeros_like(rows)
    bit, weight = devices // 2, 1
    while bit:
        place = place + jnp.where((apart & bit) != 0, weight, 0)
        bit //= 2
        weight *= 2
    return jnp.stack([place, rows % per, jnp.full_like(rows, lax.axis_index("tp"))])


def take_rows(places_ref, near_ref, far_ref):
    count, per, width = near_ref.shape
    rows = lax.broadcasted_iota(jnp.int32, (per, width), 0)
    taken = []
    table = places_ref[...]
    for i in range(table.shape[1]):
        place, row = table[0, i], table[1, i]
        near = near_ref[jnp.minimum(place, count - 1)].astype(F32)
        far = far_ref[jnp.maximum(place - count, 0)].astype(F32)
        block = jnp.where(place < count, near, far)
        taken.append(jnp.sum(jnp.where(rows == row, block, 0.0), axis=0, keepdims=True))
    return jnp.concatenate(taken, axis=0)


def sum_by_halving(kept, sent, parts):
    bit = parts // 2
    while True:
        kept = kept + lax.ppermute(sent, "tp", [(i, i ^ bit) for i in range(parts)])
        if bit == 1:
            return kept[0]
        bit //= 2
        kept, sent = kept[:bit], kept[bit:]


def rotary_factors(lengths, heads):
    rotary_dims = HS // 4
    half = rotary_dims // 2
    rates = 10000.0 ** (-2.0 * jnp.arange(half, dtype=F32) / rotary_dims)
    angle = lengths.astype(F32)[:, None] * rates[None, :]
    cosine, sine = jnp.cos(angle), jnp.sin(angle)
    rows = lengths.shape[0]
    none = jnp.zeros((rows, half), F32)
    rest = jnp.zeros((rows, HS - rotary_dims), F32)
    same = jnp.concatenate([cosine, cosine, rest + 1.0], axis=1)
    right = jnp.concatenate([-sine, none, rest], axis=1)
    left = jnp.concatenate([none, sine, rest], axis=1)
    return jnp.stack([jnp.tile(f, (1, heads)) for f in (same, right, left)])


def attend(parts, places_ref, near_ref, far_ref, factors_ref, table_ref, lengths_ref,
           keys_ref, values_ref, weight_ref, kept_out, sent_out, keys_out, values_out,
           key_ref, value_ref, sems):
    half = places_ref[...][2, 0]
    slots, width = key_ref.shape
    heads = width // HS
    pages, page = keys_ref.shape[0], keys_ref.shape[1]
    tokens = pages * page
    scale = HS ** (-0.5)

    taken = take_rows(places_ref, near_ref, far_ref)
    query, key, value = (taken[:, i * width:(i + 1) * width] for i in range(3))

    def rotate(x):
        right = pltpu.roll(x, width - HS // 8, 1)
        left = pltpu.roll(x, HS // 8, 1)
        return x * factors_ref[0] + right * factors_ref[1] + left * factors_ref[2]

    query = rotate(query).astype(BF16).astype(F32)
    key = rotate(key).astype(BF16)
    key_ref[...] = key
    value_ref[...] = value.astype(BF16)
    copies = [
        pltpu.make_async_copy(key_ref, keys_out, sems.at[0]),
        pltpu.make_async_copy(value_ref, values_out, sems.at[1]),
    ]
    for copy in copies:
        copy.start()

    rows = heads * slots
    row_head = lax.broadcasted_iota(jnp.int32, (rows, width), 0) // slots
    lane_head = lax.broadcasted_iota(jnp.int32, (rows, width), 1) // HS
    mine = row_head == lane_head
    spread_query = jnp.where(mine, jnp.concatenate([query] * heads, axis=0), 0.0)
    own_score = jnp.sum(
        spread_query * jnp.concatenate([key.astype(F32)] * heads, axis=0), axis=1, keepdims=True
    ) * scale

    lane = lax.broadcasted_iota(jnp.int32, (slots, 128), 1)
    visible = jnp.zeros((slots, 128), jnp.int32)
    for i in range(table_ref.shape[1]):
        left_over = jnp.clip(lengths_ref[...] - i * page, 0, page)
        visible = jnp.where((lane == table_ref[:, i:i + 1]) & (left_over > 0), left_over, visible)
    visible = jnp.concatenate([visible] * heads, axis=0)

    scores = lax.dot_general(
        spread_query.astype(BF16), keys_ref[...].reshape(tokens, width),
        (((1,), (1,)), ((), ())), preferred_element_type=F32,
    ) * scale
    place = lax.broadcasted_iota(jnp.int32, (rows, page), 1)
    masked = jnp.concatenate(
        [
            jnp.where(place < visible[:, p:p + 1], scores[:, p * page:(p + 1) * page], -jnp.inf)
            for p in range(pages)
        ],
        axis=1,
    )
    top = jnp.maximum(jnp.max(masked, axis=1, keepdims=True), own_score)
    exps = jnp.exp(masked - top)
    own_exp = jnp.exp(own_score - top)
    total = jnp.sum(exps, axis=1, keepdims=True) + own_exp
    share = 1.0 / total
    weights = (exps * share).astype(BF16)
    own_weight = (own_exp * share).astype(BF16).astype(F32)
    attended = jnp.dot(weights, values_ref[...].reshape(tokens, width), preferred_element_type=F32)
    attended = attended + own_weight * jnp.concatenate([value] * heads, axis=0)
    attended = jnp.where(mine, attended, 0.0)
    attended = sum(attended[h * slots:(h + 1) * slots] for h in range(heads)).astype(BF16)

    for i in range(parts):
        columns = pl.ds(pl.multiple_of((half ^ i) * width, width), width)
        out = kept_out if i < parts // 2 else sent_out
        out[i % (parts // 2)] = jnp.dot(attended, weight_ref[:, columns], preferred_element_type=F32)
    for copy in copies:
        copy.wait()


def finish(places_ref, near_ref, far_ref, residual_ref, bias_ref, out_ref):
    taken = take_rows(places_ref, near_ref, far_ref)
    out_ref[...] = (residual_ref[...].astype(F32) + bias_ref[...].astype(F32) + taken).astype(BF16)


def on_device(devices, parts, query_new, key_new, value_new, residual, dense_weight, dense_bias,
              key_pool, value_pool, page_table, lengths, request_slot, arrival_index):
    rows, width = query_new.shape
    heads = width // HS
    fresh = jnp.concatenate([query_new, key_new, value_new], axis=1)
    near, far = gather_by_doubling(fresh, devices, [0, 1 << 31, 1 << 31])
    half_terms = jax.ShapeDtypeStruct((parts // 2, rows, width), F32)
    narrow = jax.ShapeDtypeStruct((rows, width), BF16)
    kept, sent, appended_keys, appended_values = pl.pallas_call(
        functools.partial(attend, parts),
        out_shape=(half_terms, half_terms, narrow, narrow),
        in_specs=[VMEM] * 9,
        out_specs=(VMEM, VMEM, ANY, ANY),
        scratch_shapes=[
            pltpu.VMEM((rows, width), BF16),
            pltpu.VMEM((rows, width), BF16),
            pltpu.SemaphoreType.DMA((2,)),
        ],
        compiler_params=pltpu.CompilerParams(vmem_limit_bytes=8 << 20),
    )(places(arrival_index, rows, devices), near, far, rotary_factors(lengths, heads), page_table,
      lengths[:, None], key_pool, value_pool, dense_weight)
    near, far = gather_by_doubling(sum_by_halving(kept, sent, parts).astype(BF16), devices, [])
    hidden = pl.pallas_call(
        finish,
        out_shape=narrow,
        in_specs=[VMEM] * 5,
        out_specs=VMEM,
        compiler_params=pltpu.CompilerParams(vmem_limit_bytes=2 << 20),
    )(places(request_slot, rows, devices), near, far, residual, dense_bias[None, :])
    return hidden, appended_keys, appended_values


def solution(mesh):
    rows = P("req", "tp")
    pool = P("req", None, "tp")
    in_specs = (rows,) * 4 + (P("tp", None), P("tp"), pool, pool, P("req", None)) + (P("req"),) * 3
    step = functools.partial(on_device, mesh.shape["req"], mesh.shape["tp"])
    return jax.shard_map(step, mesh=mesh, in_specs=in_specs, out_specs=(rows,) * 3, check_vma=False)
```

```python
import functools

import jax
import jax.numpy as jnp
from jax import lax
from jax.experimental import pallas as pl
from jax.experimental.pallas import tpu as pltpu
from jax.sharding import PartitionSpec as P

HS = 256
BF16 = jnp.bfloat16
F32 = jnp.float32
ANY = pl.BlockSpec(memory_space=pl.ANY)
VMEM = pl.BlockSpec(memory_space=pltpu.VMEM)


def joined(own_ref, other_ref, out_ref):
    count = own_ref.shape[0]
    out_ref[:count] = own_ref[...]
    out_ref[count:] = other_ref[...]


def join(own, other, work):
    return pl.pallas_call(
        joined,
        out_shape=jax.ShapeDtypeStruct((2 * own.shape[0],) + own.shape[1:], own.dtype),
        in_specs=[VMEM, VMEM],
        out_specs=VMEM,
        cost_estimate=pl.CostEstimate(flops=work, bytes_accessed=work >> 14, transcendentals=0),
        compiler_params=pltpu.CompilerParams(vmem_limit_bytes=1 << 20),
    )(own, other)


def gather_by_doubling(block, devices, works):
    held = block[None]
    bit = devices // 2
    while True:
        other = lax.ppermute(held, "req", [(i, i ^ bit) for i in range(devices)])
        if bit == 1:
            return held, other
        held = join(held, other, works.pop(0) if works else 0)
        bit //= 2


def places(rows, per, devices):
    apart = (rows // per) ^ lax.axis_index("req").astype(jnp.int32)
    place = jnp.zeros_like(rows)
    bit, weight = devices // 2, 1
    while bit:
        place = place + jnp.where((apart & bit) != 0, weight, 0)
        bit //= 2
        weight *= 2
    return jnp.stack([place, rows % per, jnp.full_like(rows, lax.axis_index("tp"))])


def take_rows(places_ref, near_ref, far_ref):
    count, per, width = near_ref.shape
    rows = lax.broadcasted_iota(jnp.int32, (per, width), 0)
    taken = []
    table = places_ref[...]
    for i in range(table.shape[1]):
        place, row = table[0, i], table[1, i]
        near = near_ref[jnp.minimum(place, count - 1)].astype(F32)
        far = far_ref[jnp.maximum(place - count, 0)].astype(F32)
        block = jnp.where(place < count, near, far)
        taken.append(jnp.sum(jnp.where(rows == row, block, 0.0), axis=0, keepdims=True))
    return jnp.concatenate(taken, axis=0)


def sum_by_halving(kept, sent, parts):
    bit = parts // 2
    while True:
        kept = kept + lax.ppermute(sent, "tp", [(i, i ^ bit) for i in range(parts)])
        if bit == 1:
            return kept[0]
        bit //= 2
        kept, sent = kept[:bit], kept[bit:]


def rotary_factors(lengths, heads):
    rotary_dims = HS // 4
    half = rotary_dims // 2
    rates = 10000.0 ** (-2.0 * jnp.arange(half, dtype=F32) / rotary_dims)
    angle = lengths.astype(F32)[:, None] * rates[None, :]
    cosine, sine = jnp.cos(angle), jnp.sin(angle)
    rows = lengths.shape[0]
    none = jnp.zeros((rows, half), F32)
    rest = jnp.zeros((rows, HS - rotary_dims), F32)
    same = jnp.concatenate([cosine, cosine, rest + 1.0], axis=1)
    right = jnp.concatenate([-sine, none, rest], axis=1)
    left = jnp.concatenate([none, sine, rest], axis=1)
    return jnp.stack([jnp.tile(f, (1, heads)) for f in (same, right, left)])


def attend(parts, places_ref, near_ref, far_ref, factors_ref, table_ref, lengths_ref,
           keys_ref, values_ref, weight_ref, kept_out, sent_out, keys_out, values_out,
           key_ref, value_ref, sems):
    half = places_ref[...][2, 0]
    slots, width = key_ref.shape
    heads = width // HS
    pages, page = keys_ref.shape[0], keys_ref.shape[1]
    tokens = pages * page
    scale = HS ** (-0.5)

    taken = take_rows(places_ref, near_ref, far_ref)
    query, key, value = (taken[:, i * width:(i + 1) * width] for i in range(3))

    def rotate(x):
        right = pltpu.roll(x, width - HS // 8, 1)
        left = pltpu.roll(x, HS // 8, 1)
        return x * factors_ref[0] + right * factors_ref[1] + left * factors_ref[2]

    query = rotate(query).astype(BF16).astype(F32)
    key = rotate(key).astype(BF16)
    key_ref[...] = key
    value_ref[...] = value.astype(BF16)
    copies = [
        pltpu.make_async_copy(key_ref, keys_out, sems.at[0]),
        pltpu.make_async_copy(value_ref, values_out, sems.at[1]),
    ]
    for copy in copies:
        copy.start()

    rows = heads * slots
    row_head = lax.broadcasted_iota(jnp.int32, (rows, width), 0) // slots
    lane_head = lax.broadcasted_iota(jnp.int32, (rows, width), 1) // HS
    mine = row_head == lane_head
    spread_query = jnp.where(mine, jnp.concatenate([query] * heads, axis=0), 0.0)
    own_score = jnp.sum(
        spread_query * jnp.concatenate([key.astype(F32)] * heads, axis=0), axis=1, keepdims=True
    ) * scale

    lane = lax.broadcasted_iota(jnp.int32, (slots, 128), 1)
    visible = jnp.zeros((slots, 128), jnp.int32)
    for i in range(table_ref.shape[1]):
        left_over = jnp.clip(lengths_ref[...] - i * page, 0, page)
        visible = jnp.where((lane == table_ref[:, i:i + 1]) & (left_over > 0), left_over, visible)
    visible = jnp.concatenate([visible] * heads, axis=0)

    scores = lax.dot_general(
        spread_query.astype(BF16), keys_ref[...].reshape(tokens, width),
        (((1,), (1,)), ((), ())), preferred_element_type=F32,
    ) * scale
    place = lax.broadcasted_iota(jnp.int32, (rows, page), 1)
    masked = jnp.concatenate(
        [
            jnp.where(place < visible[:, p:p + 1], scores[:, p * page:(p + 1) * page], -jnp.inf)
            for p in range(pages)
        ],
        axis=1,
    )
    top = jnp.maximum(jnp.max(masked, axis=1, keepdims=True), own_score)
    exps = jnp.exp(masked - top)
    own_exp = jnp.exp(own_score - top)
    total = jnp.sum(exps, axis=1, keepdims=True) + own_exp
    share = 1.0 / total
    weights = (exps * share).astype(BF16)
    own_weight = (own_exp * share).astype(BF16).astype(F32)
    attended = jnp.dot(weights, values_ref[...].reshape(tokens, width), preferred_element_type=F32)
    attended = attended + own_weight * jnp.concatenate([value] * heads, axis=0)
    attended = jnp.where(mine, attended, 0.0)
    attended = sum(attended[h * slots:(h + 1) * slots] for h in range(heads)).astype(BF16)

    for i in range(parts):
        columns = pl.ds(pl.multiple_of((half ^ i) * width, width), width)
        out = kept_out if i < parts // 2 else sent_out
        out[i % (parts // 2)] = jnp.dot(attended, weight_ref[:, columns], preferred_element_type=F32)
    for copy in copies:
        copy.wait()


def finish(places_ref, near_ref, far_ref, residual_ref, bias_ref, out_ref):
    taken = take_rows(places_ref, near_ref, far_ref)
    out_ref[...] = (residual_ref[...].astype(F32) + bias_ref[...].astype(F32) + taken).astype(BF16)


def on_device(devices, parts, query_new, key_new, value_new, residual, dense_weight, dense_bias,
              key_pool, value_pool, page_table, lengths, request_slot, arrival_index):
    rows, width = query_new.shape
    heads = width // HS
    fresh = jnp.concatenate([query_new, key_new, value_new], axis=1)
    near, far = gather_by_doubling(fresh, devices, [0, 3 << 30, 1 << 31])
    half_terms = jax.ShapeDtypeStruct((parts // 2, rows, width), F32)
    narrow = jax.ShapeDtypeStruct((rows, width), BF16)
    kept, sent, appended_keys, appended_values = pl.pallas_call(
        functools.partial(attend, parts),
        out_shape=(half_terms, half_terms, narrow, narrow),
        in_specs=[VMEM] * 9,
        out_specs=(VMEM, VMEM, ANY, ANY),
        scratch_shapes=[
            pltpu.VMEM((rows, width), BF16),
            pltpu.VMEM((rows, width), BF16),
            pltpu.SemaphoreType.DMA((2,)),
        ],
        compiler_params=pltpu.CompilerParams(vmem_limit_bytes=8 << 20),
    )(places(arrival_index, rows, devices), near, far, rotary_factors(lengths, heads), page_table,
      lengths[:, None], key_pool, value_pool, dense_weight)
    near, far = gather_by_doubling(sum_by_halving(kept, sent, parts).astype(BF16), devices, [])
    hidden = pl.pallas_call(
        finish,
        out_shape=narrow,
        in_specs=[VMEM] * 5,
        out_specs=VMEM,
        compiler_params=pltpu.CompilerParams(vmem_limit_bytes=2 << 20),
    )(places(request_slot, rows, devices), near, far, residual, dense_bias[None, :])
    return hidden, appended_keys, appended_values


def solution(mesh):
    rows = P("req", "tp")
    pool = P("req", None, "tp")
    in_specs = (rows,) * 4 + (P("tp", None), P("tp"), pool, pool, P("req", None)) + (P("req"),) * 3
    step = functools.partial(on_device, mesh.shape["req"], mesh.shape["tp"])
    return jax.shard_map(step, mesh=mesh, in_specs=in_specs, out_specs=(rows,) * 3, check_vma=False)
```

```python
import functools

import jax
import jax.numpy as jnp
from jax import lax
from jax.experimental import pallas as pl
from jax.experimental.pallas import tpu as pltpu
from jax.sharding import PartitionSpec as P

HS = 256
TURN = 4<<30
BF16 = jnp.bfloat16
F32 = jnp.float32
ANY = pl.BlockSpec(memory_space=pl.ANY)
VMEM = pl.BlockSpec(memory_space=pltpu.VMEM)


def joined(own_ref, other_ref, *rest):
    out_ref = rest[-1]
    count = own_ref.shape[0]
    out_ref[:count] = own_ref[...]
    out_ref[count:] = other_ref[...]


def join(own, other, work, *first):
    return pl.pallas_call(
        joined,
        out_shape=jax.ShapeDtypeStruct((2 * own.shape[0],) + own.shape[1:], own.dtype),
        in_specs=[VMEM, VMEM] + [ANY] * len(first),
        out_specs=VMEM,
        cost_estimate=pl.CostEstimate(flops=work, bytes_accessed=work >> 14, transcendentals=0),
        compiler_params=pltpu.CompilerParams(vmem_limit_bytes=1 << 20),
    )(own, other, *first)


def gather_by_doubling(block, devices, works, beside=None):
    held = block[None]
    bit = devices // 2
    extra = ()
    while True:
        other = lax.ppermute(held, "req", [(i, i ^ bit) for i in range(devices)])
        if bit == 1:
            return (held, other) + extra
        if bit == 2 and beside is not None:
            extra = (beside(held),)
        held = join(held, other, works.pop(0) if works else 0, *extra)
        bit //= 2


def places(rows, per, devices):
    apart = (rows // per) ^ lax.axis_index("req").astype(jnp.int32)
    place = jnp.zeros_like(rows)
    bit, weight = devices // 2, 1
    while bit:
        place = place + jnp.where((apart & bit) != 0, weight, 0)
        bit //= 2
        weight *= 2
    return jnp.stack([place, rows % per, jnp.full_like(rows, lax.axis_index("tp"))])


def take_rows(places_ref, near_ref, far_ref):
    count, per, width = near_ref.shape
    rows = lax.broadcasted_iota(jnp.int32, (per, width), 0)
    taken = []
    table = places_ref[...]
    for i in range(table.shape[1]):
        place, row = table[0, i], table[1, i]
        near = near_ref[jnp.minimum(place, count - 1)].astype(F32)
        far = far_ref[jnp.maximum(place - count, 0)].astype(F32)
        block = jnp.where(place < count, near, far)
        taken.append(jnp.sum(jnp.where(rows == row, block, 0.0), axis=0, keepdims=True))
    return jnp.concatenate(taken, axis=0)


def sum_by_halving(kept, sent, parts):
    bit = parts // 2
    while True:
        kept = kept + lax.ppermute(sent, "tp", [(i, i ^ bit) for i in range(parts)])
        if bit == 1:
            return kept[0]
        bit //= 2
        kept, sent = kept[:bit], kept[bit:]


def rotary_factors(lengths, heads):
    rotary_dims = HS // 4
    half = rotary_dims // 2
    rates = 10000.0 ** (-2.0 * jnp.arange(half, dtype=F32) / rotary_dims)
    angle = lengths.astype(F32)[:, None] * rates[None, :]
    cosine, sine = jnp.cos(angle), jnp.sin(angle)
    rows = lengths.shape[0]
    none = jnp.zeros((rows, half), F32)
    rest = jnp.zeros((rows, HS - rotary_dims), F32)
    same = jnp.concatenate([cosine, cosine, rest + 1.0], axis=1)
    right = jnp.concatenate([-sine, none, rest], axis=1)
    left = jnp.concatenate([none, sine, rest], axis=1)
    return jnp.stack([jnp.tile(f, (1, heads)) for f in (same, right, left)])


def turn(pages_ref, after_ref, out_ref):
    pages, page, _ = pages_ref.shape
    for p in range(pages):
        out_ref[:, p * page:(p + 1) * page] = pages_ref[p].T


def turned(pool, after):
    pages, page, width = pool.shape
    return pl.pallas_call(
        turn,
        out_shape=jax.ShapeDtypeStruct((width, pages * page), pool.dtype),
        in_specs=[VMEM, ANY],
        out_specs=VMEM,
        cost_estimate=pl.CostEstimate(flops=TURN, bytes_accessed=1 << 20, transcendentals=0),
        compiler_params=pltpu.CompilerParams(vmem_limit_bytes=8 << 20),
    )(pool, after)


def attend(parts, places_ref, near_ref, far_ref, factors_ref, table_ref, lengths_ref,
           keys_ref, values_ref, weight_ref, kept_out, sent_out, keys_out, values_out,
           key_ref, value_ref, sems):
    half = places_ref[...][2, 0]
    slots, width = key_ref.shape
    heads = width // HS
    pages, page = values_ref.shape[0], values_ref.shape[1]
    tokens = pages * page
    scale = HS ** (-0.5)

    taken = take_rows(places_ref, near_ref, far_ref)
    query, key, value = (taken[:, i * width:(i + 1) * width] for i in range(3))

    def rotate(x):
        right = pltpu.roll(x, width - HS // 8, 1)
        left = pltpu.roll(x, HS // 8, 1)
        return x * factors_ref[0] + right * factors_ref[1] + left * factors_ref[2]

    query = rotate(query).astype(BF16).astype(F32)
    key = rotate(key).astype(BF16)
    key_ref[...] = key
    value_ref[...] = value.astype(BF16)
    copies = [
        pltpu.make_async_copy(key_ref, keys_out, sems.at[0]),
        pltpu.make_async_copy(value_ref, values_out, sems.at[1]),
    ]
    for copy in copies:
        copy.start()

    rows = heads * slots
    row_head = lax.broadcasted_iota(jnp.int32, (rows, width), 0) // slots
    lane_head = lax.broadcasted_iota(jnp.int32, (rows, width), 1) // HS
    mine = row_head == lane_head
    spread_query = jnp.where(mine, jnp.concatenate([query] * heads, axis=0), 0.0)
    own_score = jnp.sum(
        spread_query * jnp.concatenate([key.astype(F32)] * heads, axis=0), axis=1, keepdims=True
    ) * scale

    lane = lax.broadcasted_iota(jnp.int32, (slots, 128), 1)
    visible = jnp.zeros((slots, 128), jnp.int32)
    for i in range(table_ref.shape[1]):
        left_over = jnp.clip(lengths_ref[...] - i * page, 0, page)
        visible = jnp.where((lane == table_ref[:, i:i + 1]) & (left_over > 0), left_over, visible)
    visible = jnp.concatenate([visible] * heads, axis=0)

    queries = spread_query.astype(BF16)
    place = lax.broadcasted_iota(jnp.int32, (rows, page), 1)
    step = next(n for n in (24, 4, 2, 1) if pages % n == 0)
    tops, sums, parts_seen = [], [], []
    for first in range(0, pages, step):
        scores = jnp.dot(queries, keys_ref[:, first * page:(first + step) * page], preferred_element_type=F32) * scale
        masked = jnp.concatenate(
            [
                jnp.where(place < visible[:, first + p:first + p + 1], scores[:, p * page:(p + 1) * page], -jnp.inf)
                for p in range(step)
            ],
            axis=1,
        )
        top = jnp.maximum(jnp.max(masked, axis=1, keepdims=True), own_score)
        exps = jnp.exp(masked - top)
        tops.append(top)
        sums.append(jnp.sum(exps, axis=1, keepdims=True))
        parts_seen.append(
            jnp.dot(exps.astype(BF16), values_ref[first:first + step].reshape(step * page, width), preferred_element_type=F32)
        )
    top = functools.reduce(jnp.maximum, tops)
    own_exp = jnp.exp(own_score - top)
    total = own_exp
    attended = own_exp * jnp.concatenate([value] * heads, axis=0)
    for group_top, group_sum, seen in zip(tops, sums, parts_seen):
        factor = jnp.exp(group_top - top)
        total = total + factor * group_sum
        attended = attended + factor * seen
    attended = attended * (1.0 / total)
    attended = jnp.where(mine, attended, 0.0)
    attended = sum(attended[h * slots:(h + 1) * slots] for h in range(heads)).astype(BF16)

    for i in range(parts):
        columns = pl.ds(pl.multiple_of((half ^ i) * width, width), width)
        out = kept_out if i < parts // 2 else sent_out
        out[i % (parts // 2)] = jnp.dot(attended, weight_ref[:, columns], preferred_element_type=F32)
    for copy in copies:
        copy.wait()


def finish(places_ref, near_ref, far_ref, residual_ref, bias_ref, out_ref):
    taken = take_rows(places_ref, near_ref, far_ref)
    out_ref[...] = (residual_ref[...].astype(F32) + bias_ref[...].astype(F32) + taken).astype(BF16)


def on_device(devices, parts, query_new, key_new, value_new, residual, dense_weight, dense_bias,
              key_pool, value_pool, page_table, lengths, request_slot, arrival_index):
    rows, width = query_new.shape
    heads = width // HS
    fresh = jnp.concatenate([query_new, key_new, value_new], axis=1)
    near, far, keys = gather_by_doubling(fresh, devices, [0,6<<30,2<<30], functools.partial(turned, key_pool))
    half_terms = jax.ShapeDtypeStruct((parts // 2, rows, width), F32)
    narrow = jax.ShapeDtypeStruct((rows, width), BF16)
    kept, sent, appended_keys, appended_values = pl.pallas_call(
        functools.partial(attend, parts),
        out_shape=(half_terms, half_terms, narrow, narrow),
        in_specs=[VMEM] * 9,
        out_specs=(VMEM, VMEM, ANY, ANY),
        scratch_shapes=[
            pltpu.VMEM((rows, width), BF16),
            pltpu.VMEM((rows, width), BF16),
            pltpu.SemaphoreType.DMA((2,)),
        ],
        compiler_params=pltpu.CompilerParams(vmem_limit_bytes=8 << 20),
    )(places(arrival_index, rows, devices), near, far, rotary_factors(lengths, heads), page_table,
      lengths[:, None], keys, value_pool, dense_weight)
    near, far = gather_by_doubling(sum_by_halving(kept, sent, parts).astype(BF16), devices, [])
    hidden = pl.pallas_call(
        finish,
        out_shape=narrow,
        in_specs=[VMEM] * 5,
        out_specs=VMEM,
        compiler_params=pltpu.CompilerParams(vmem_limit_bytes=2 << 20),
    )(places(request_slot, rows, devices), near, far, residual, dense_bias[None, :])
    return hidden, appended_keys, appended_values


def solution(mesh):
    rows = P("req", "tp")
    pool = P("req", None, "tp")
    in_specs = (rows,) * 4 + (P("tp", None), P("tp"), pool, pool, P("req", None)) + (P("req"),) * 3
    step = functools.partial(on_device, mesh.shape["req"], mesh.shape["tp"])
    return jax.shard_map(step, mesh=mesh, in_specs=in_specs, out_specs=(rows,) * 3, check_vma=False)
```

```python
import functools

import jax
import jax.numpy as jnp
from jax import lax
from jax.experimental import pallas as pl
from jax.experimental.pallas import tpu as pltpu
from jax.sharding import PartitionSpec as P

HS = 256
TURN = 4<<30
BF16 = jnp.bfloat16
F32 = jnp.float32
ANY = pl.BlockSpec(memory_space=pl.ANY)
VMEM = pl.BlockSpec(memory_space=pltpu.VMEM)


def joined(own_ref, other_ref, *rest):
    out_ref = rest[-1]
    count = own_ref.shape[0]
    out_ref[:count] = own_ref[...]
    out_ref[count:] = other_ref[...]


def join(own, other, work, *first):
    return pl.pallas_call(
        joined,
        out_shape=jax.ShapeDtypeStruct((2 * own.shape[0],) + own.shape[1:], own.dtype),
        in_specs=[VMEM, VMEM] + [ANY] * len(first),
        out_specs=VMEM,
        cost_estimate=pl.CostEstimate(flops=work, bytes_accessed=work >> 14, transcendentals=0),
        compiler_params=pltpu.CompilerParams(vmem_limit_bytes=1 << 20),
    )(own, other, *first)


def gather_by_doubling(block, devices, works, beside=None):
    held = block[None]
    bit = devices // 2
    extra = ()
    while True:
        other = lax.ppermute(held, "req", [(i, i ^ bit) for i in range(devices)])
        if bit == 1:
            return (held, other) + extra
        if bit == 2 and beside is not None:
            extra = (beside(held),)
        held = join(held, other, works.pop(0) if works else 0, *extra)
        bit //= 2


def places(rows, per, devices):
    apart = (rows // per) ^ lax.axis_index("req").astype(jnp.int32)
    place = jnp.zeros_like(rows)
    bit, weight = devices // 2, 1
    while bit:
        place = place + jnp.where((apart & bit) != 0, weight, 0)
        bit //= 2
        weight *= 2
    return jnp.stack([place, rows % per, jnp.full_like(rows, lax.axis_index("tp"))])


def take_rows(places_ref, near_ref, far_ref):
    count, per, width = near_ref.shape
    rows = lax.broadcasted_iota(jnp.int32, (per, width), 0)
    taken = []
    table = places_ref[...]
    for i in range(table.shape[1]):
        place, row = table[0, i], table[1, i]
        near = near_ref[jnp.minimum(place, count - 1)].astype(F32)
        far = far_ref[jnp.maximum(place - count, 0)].astype(F32)
        block = jnp.where(place < count, near, far)
        taken.append(jnp.sum(jnp.where(rows == row, block, 0.0), axis=0, keepdims=True))
    return jnp.concatenate(taken, axis=0)


def sum_by_halving(kept, sent, parts):
    bit = parts // 2
    while True:
        kept = kept + lax.ppermute(sent, "tp", [(i, i ^ bit) for i in range(parts)]).astype(F32)
        if bit == 1:
            return kept[0]
        bit //= 2
        kept, sent = kept[:bit], kept[bit:].astype(BF16)


def rotary_factors(lengths, heads):
    rotary_dims = HS // 4
    half = rotary_dims // 2
    rates = 10000.0 ** (-2.0 * jnp.arange(half, dtype=F32) / rotary_dims)
    angle = lengths.astype(F32)[:, None] * rates[None, :]
    cosine, sine = jnp.cos(angle), jnp.sin(angle)
    rows = lengths.shape[0]
    none = jnp.zeros((rows, half), F32)
    rest = jnp.zeros((rows, HS - rotary_dims), F32)
    same = jnp.concatenate([cosine, cosine, rest + 1.0], axis=1)
    right = jnp.concatenate([-sine, none, rest], axis=1)
    left = jnp.concatenate([none, sine, rest], axis=1)
    return jnp.stack([jnp.tile(f, (1, heads)) for f in (same, right, left)])


def turn(pages_ref, after_ref, out_ref):
    pages, page, _ = pages_ref.shape
    for p in range(pages):
        out_ref[:, p * page:(p + 1) * page] = pages_ref[p].T


def turned(pool, after):
    pages, page, width = pool.shape
    return pl.pallas_call(
        turn,
        out_shape=jax.ShapeDtypeStruct((width, pages * page), pool.dtype),
        in_specs=[VMEM, ANY],
        out_specs=VMEM,
        cost_estimate=pl.CostEstimate(flops=TURN, bytes_accessed=1 << 20, transcendentals=0),
        compiler_params=pltpu.CompilerParams(vmem_limit_bytes=8 << 20),
    )(pool, after)


def project(attended, weight_ref, part):
    width = attended.shape[1]
    columns = pl.ds(pl.multiple_of(part * width, width), width)
    return jnp.dot(attended, weight_ref[:, columns], preferred_element_type=F32)


def attend(parts, places_ref, near_ref, far_ref, factors_ref, table_ref, lengths_ref,
           keys_ref, values_ref, weight_ref, attended_out, sent_out, keys_out, values_out,
           key_ref, value_ref, sems):
    half = places_ref[...][2, 0]
    slots, width = key_ref.shape
    heads = width // HS
    pages, page = values_ref.shape[0], values_ref.shape[1]
    tokens = pages * page
    scale = HS ** (-0.5)

    taken = take_rows(places_ref, near_ref, far_ref)
    query, key, value = (taken[:, i * width:(i + 1) * width] for i in range(3))

    def rotate(x):
        right = pltpu.roll(x, width - HS // 8, 1)
        left = pltpu.roll(x, HS // 8, 1)
        return x * factors_ref[0] + right * factors_ref[1] + left * factors_ref[2]

    query = rotate(query).astype(BF16).astype(F32)
    key = rotate(key).astype(BF16)
    key_ref[...] = key
    value_ref[...] = value.astype(BF16)
    copies = [
        pltpu.make_async_copy(key_ref, keys_out, sems.at[0]),
        pltpu.make_async_copy(value_ref, values_out, sems.at[1]),
    ]
    for copy in copies:
        copy.start()

    lane = lax.broadcasted_iota(jnp.int32, (slots, 128), 1)
    visible = jnp.zeros((slots, 128), jnp.int32)
    for i in range(table_ref.shape[1]):
        left_over = jnp.clip(lengths_ref[...] - i * page, 0, page)
        visible = jnp.where((lane == table_ref[:, i:i + 1]) & (left_over > 0), left_over, visible)

    together = min(1, heads)
    rows, lanes = together * slots, together * HS
    row_head = lax.broadcasted_iota(jnp.int32, (rows, lanes), 0) // slots
    lane_head = lax.broadcasted_iota(jnp.int32, (rows, lanes), 1) // HS
    mine = row_head == lane_head
    place = lax.broadcasted_iota(jnp.int32, (rows, page), 1)
    shown = jnp.concatenate([visible] * together, axis=0)
    shown = [place < shown[:, p:p + 1] for p in range(pages)]
    attended = []
    for first in range(0, width, lanes):
        spread = [jnp.concatenate([x[:, first:first + lanes]] * together, axis=0) for x in (query, key.astype(F32), value)]
        queries = jnp.where(mine, spread[0], 0.0)
        own_score = jnp.sum(queries * spread[1], axis=1, keepdims=True) * scale
        scores = jnp.dot(queries.astype(BF16), keys_ref[first:first + lanes], preferred_element_type=F32) * scale
        masked = jnp.concatenate(
            [jnp.where(shown[p], scores[:, p * page:(p + 1) * page], -jnp.inf) for p in range(pages)], axis=1
        )
        top = jnp.maximum(jnp.max(masked, axis=1, keepdims=True), own_score)
        exps = jnp.exp(masked - top)
        own_exp = jnp.exp(own_score - top)
        total = jnp.sum(exps, axis=1, keepdims=True) + own_exp
        seen = jnp.dot(
            exps.astype(BF16),
            values_ref[:, :, first:first + lanes].reshape(tokens, lanes),
            preferred_element_type=F32,
        )
        seen = jnp.where(mine, (seen + own_exp * spread[2]) * (1.0 / total), 0.0)
        attended.append(sum(seen[h * slots:(h + 1) * slots] for h in range(together)))
    attended = jnp.concatenate(attended, axis=1).astype(BF16)

    attended_out[...] = attended
    for i in range(parts // 2):
        sent_out[i] = project(attended, weight_ref, half ^ (parts // 2 + i)).astype(BF16)
    for copy in copies:
        copy.wait()


def keep(parts, places_ref, attended_ref, weight_ref, kept_out):
    for i in range(parts // 2):
        kept_out[i] = project(attended_ref[...], weight_ref, places_ref[...][2, 0] ^ i)


def finish(places_ref, near_ref, far_ref, residual_ref, bias_ref, out_ref):
    taken = take_rows(places_ref, near_ref, far_ref)
    out_ref[...] = (residual_ref[...].astype(F32) + bias_ref[...].astype(F32) + taken).astype(BF16)


def on_device(devices, parts, query_new, key_new, value_new, residual, dense_weight, dense_bias,
              key_pool, value_pool, page_table, lengths, request_slot, arrival_index):
    rows, width = query_new.shape
    heads = width // HS
    fresh = jnp.concatenate([query_new, key_new, value_new], axis=1)
    near, far, keys = gather_by_doubling(fresh, devices, [0,6<<30,2<<30], functools.partial(turned, key_pool))
    narrow = jax.ShapeDtypeStruct((rows, width), BF16)
    where = places(arrival_index, rows, devices)
    attended, sent, appended_keys, appended_values = pl.pallas_call(
        functools.partial(attend, parts),
        out_shape=(narrow, jax.ShapeDtypeStruct((parts // 2, rows, width), BF16), narrow, narrow),
        in_specs=[VMEM] * 9,
        out_specs=(VMEM, VMEM, ANY, ANY),
        scratch_shapes=[
            pltpu.VMEM((rows, width), BF16),
            pltpu.VMEM((rows, width), BF16),
            pltpu.SemaphoreType.DMA((2,)),
        ],
        compiler_params=pltpu.CompilerParams(vmem_limit_bytes=8 << 20),
    )(where, near, far, rotary_factors(lengths, heads), page_table, lengths[:, None], keys, value_pool, dense_weight)
    kept = pl.pallas_call(
        functools.partial(keep, parts),
        out_shape=jax.ShapeDtypeStruct((parts // 2, rows, width), F32),
        in_specs=[VMEM] * 3,
        out_specs=VMEM,
        cost_estimate=pl.CostEstimate(flops=1 << 30, bytes_accessed=1 << 20, transcendentals=0),
        compiler_params=pltpu.CompilerParams(vmem_limit_bytes=8 << 20),
    )(where, attended, dense_weight)
    near, far = gather_by_doubling(sum_by_halving(kept, sent, parts).astype(BF16), devices, [])
    hidden = pl.pallas_call(
        finish,
        out_shape=narrow,
        in_specs=[VMEM] * 5,
        out_specs=VMEM,
        compiler_params=pltpu.CompilerParams(vmem_limit_bytes=2 << 20),
    )(places(request_slot, rows, devices), near, far, residual, dense_bias[None, :])
    return hidden, appended_keys, appended_values


def solution(mesh):
    rows = P("req", "tp")
    pool = P("req", None, "tp")
    in_specs = (rows,) * 4 + (P("tp", None), P("tp"), pool, pool, P("req", None)) + (P("req"),) * 3
    step = functools.partial(on_device, mesh.shape["req"], mesh.shape["tp"])
    return jax.shard_map(step, mesh=mesh, in_specs=in_specs, out_specs=(rows,) * 3, check_vma=False)
```

```python
import functools

import jax
import jax.numpy as jnp
from jax import lax
from jax.experimental import pallas as pl
from jax.experimental.pallas import tpu as pltpu
from jax.sharding import PartitionSpec as P

HS = 256
TURN = 4<<30
BF16 = jnp.bfloat16
F32 = jnp.float32
ANY = pl.BlockSpec(memory_space=pl.ANY)
VMEM = pl.BlockSpec(memory_space=pltpu.VMEM)


def joined(own_ref, other_ref, *rest):
    out_ref = rest[-1]
    count = own_ref.shape[0]
    out_ref[:count] = own_ref[...]
    out_ref[count:] = other_ref[...]


def join(own, other, work, *first):
    return pl.pallas_call(
        joined,
        out_shape=jax.ShapeDtypeStruct((2 * own.shape[0],) + own.shape[1:], own.dtype),
        in_specs=[VMEM, VMEM] + [ANY] * len(first),
        out_specs=VMEM,
        cost_estimate=pl.CostEstimate(flops=work, bytes_accessed=work >> 14, transcendentals=0),
        compiler_params=pltpu.CompilerParams(vmem_limit_bytes=1 << 20),
    )(own, other, *first)


def gather_by_doubling(block, devices, works, beside=None):
    held = block[None]
    bit = devices // 2
    extra = ()
    while True:
        other = lax.ppermute(held, "req", [(i, i ^ bit) for i in range(devices)])
        if bit == 1:
            return (held, other) + extra
        if bit == 2 and beside is not None:
            extra = (beside(held),)
        held = join(held, other, works.pop(0) if works else 0, *extra)
        bit //= 2


def places(rows, per, devices):
    apart = (rows // per) ^ lax.axis_index("req").astype(jnp.int32)
    place = jnp.zeros_like(rows)
    bit, weight = devices // 2, 1
    while bit:
        place = place + jnp.where((apart & bit) != 0, weight, 0)
        bit //= 2
        weight *= 2
    return jnp.stack([place, rows % per, jnp.full_like(rows, lax.axis_index("tp"))])


def take_rows(places_ref, near_ref, far_ref):
    count, per, width = near_ref.shape
    rows = lax.broadcasted_iota(jnp.int32, (per, width), 0)
    taken = []
    table = places_ref[...]
    for i in range(table.shape[1]):
        place, row = table[0, i], table[1, i]
        near = near_ref[jnp.minimum(place, count - 1)].astype(F32)
        far = far_ref[jnp.maximum(place - count, 0)].astype(F32)
        block = jnp.where(place < count, near, far)
        taken.append(jnp.sum(jnp.where(rows == row, block, 0.0), axis=0, keepdims=True))
    return jnp.concatenate(taken, axis=0)


def sum_by_halving(kept, sent, parts):
    bit = parts // 2
    while True:
        kept = kept + lax.ppermute(sent, "tp", [(i, i ^ bit) for i in range(parts)]).astype(F32)
        if bit == 1:
            return kept[0]
        bit //= 2
        kept, sent = kept[:bit], kept[bit:].astype(BF16)


def rotary_factors(lengths, heads):
    rotary_dims = HS // 4
    half = rotary_dims // 2
    rates = 10000.0 ** (-2.0 * jnp.arange(half, dtype=F32) / rotary_dims)
    angle = lengths.astype(F32)[:, None] * rates[None, :]
    cosine, sine = jnp.cos(angle), jnp.sin(angle)
    rows = lengths.shape[0]
    none = jnp.zeros((rows, half), F32)
    rest = jnp.zeros((rows, HS - rotary_dims), F32)
    same = jnp.concatenate([cosine, cosine, rest + 1.0], axis=1)
    right = jnp.concatenate([-sine, none, rest], axis=1)
    left = jnp.concatenate([none, sine, rest], axis=1)
    return jnp.stack([jnp.tile(f, (1, heads)) for f in (same, right, left)])


def turn(pages_ref, after_ref, out_ref):
    pages, page, _ = pages_ref.shape
    for p in range(pages):
        out_ref[:, p * page:(p + 1) * page] = pages_ref[p].T


def turned(pool, after):
    pages, page, width = pool.shape
    return pl.pallas_call(
        turn,
        out_shape=jax.ShapeDtypeStruct((width, pages * page), pool.dtype),
        in_specs=[VMEM, ANY],
        out_specs=VMEM,
        cost_estimate=pl.CostEstimate(flops=TURN, bytes_accessed=1 << 20, transcendentals=0),
        compiler_params=pltpu.CompilerParams(vmem_limit_bytes=8 << 20),
    )(pool, after)


def project(attended, weight_ref, part):
    width = attended.shape[1]
    columns = pl.ds(pl.multiple_of(part * width, width), width)
    return jnp.dot(attended, weight_ref[:, columns], preferred_element_type=F32)


def attend(parts, places_ref, near_ref, far_ref, factors_ref, table_ref, lengths_ref,
           keys_ref, values_ref, weight_ref, attended_out, sent_out, keys_out, values_out,
           key_ref, value_ref, sems):
    half = places_ref[...][2, 0]
    slots, width = key_ref.shape
    heads = width // HS
    pages, page = values_ref.shape[0], values_ref.shape[1]
    tokens = pages * page
    scale = HS ** (-0.5)

    taken = take_rows(places_ref, near_ref, far_ref)
    query, key, value = (taken[:, i * width:(i + 1) * width] for i in range(3))

    def rotate(x):
        right = pltpu.roll(x, width - HS // 8, 1)
        left = pltpu.roll(x, HS // 8, 1)
        return x * factors_ref[0] + right * factors_ref[1] + left * factors_ref[2]

    query = rotate(query).astype(BF16).astype(F32)
    key = rotate(key).astype(BF16)
    key_ref[...] = key
    value_ref[...] = value.astype(BF16)
    copies = [
        pltpu.make_async_copy(key_ref, keys_out, sems.at[0]),
        pltpu.make_async_copy(value_ref, values_out, sems.at[1]),
    ]
    for copy in copies:
        copy.start()

    lane = lax.broadcasted_iota(jnp.int32, (slots, 128), 1)
    visible = jnp.zeros((slots, 128), jnp.int32)
    for i in range(table_ref.shape[1]):
        left_over = jnp.clip(lengths_ref[...] - i * page, 0, page)
        visible = jnp.where((lane == table_ref[:, i:i + 1]) & (left_over > 0), left_over, visible)

    together = min(2, heads)
    rows, lanes = together * slots, together * HS
    row_head = lax.broadcasted_iota(jnp.int32, (rows, lanes), 0) // slots
    lane_head = lax.broadcasted_iota(jnp.int32, (rows, lanes), 1) // HS
    mine = row_head == lane_head
    place = lax.broadcasted_iota(jnp.int32, (rows, page), 1)
    shown = jnp.concatenate([visible] * together, axis=0)
    shown = [place < shown[:, p:p + 1] for p in range(pages)]
    starts = range(0, width, lanes)

    def score(first):
        spread = [jnp.concatenate([x[:, first:first + lanes]] * together, axis=0) for x in (query, key.astype(F32), value)]
        queries = jnp.where(mine, spread[0], 0.0)
        own_score = jnp.sum(queries * spread[1], axis=1, keepdims=True) * scale
        return jnp.dot(queries.astype(BF16), keys_ref[first:first + lanes], preferred_element_type=F32), own_score, spread[2]

    def soften(scores, own_score, own_value):
        masked = jnp.concatenate(
            [jnp.where(shown[p], scores[:, p * page:(p + 1) * page] * scale, -jnp.inf) for p in range(pages)], axis=1
        )
        top = jnp.maximum(jnp.max(masked, axis=1, keepdims=True), own_score)
        exps = jnp.exp(masked - top)
        own_exp = jnp.exp(own_score - top)
        total = jnp.sum(exps, axis=1, keepdims=True) + own_exp
        return exps.astype(BF16), own_exp * own_value, 1.0 / total

    def gather_values(first, exps, own, share):
        seen = jnp.dot(exps, values_ref[:, :, first:first + lanes].reshape(tokens, lanes), preferred_element_type=F32)
        seen = jnp.where(mine, (seen + own) * share, 0.0)
        return sum(seen[h * slots:(h + 1) * slots] for h in range(together))

    scored = [score(first) for first in starts]
    softened = [soften(*x) for x in scored]
    attended = [gather_values(first, *x) for first, x in zip(starts, softened)]
    attended = jnp.concatenate(attended, axis=1).astype(BF16)

    attended_out[...] = attended
    for i in range(parts // 2):
        sent_out[i] = project(attended, weight_ref, half ^ (parts // 2 + i)).astype(BF16)
    for copy in copies:
        copy.wait()


def keep(parts, places_ref, attended_ref, weight_ref, kept_out):
    for i in range(parts // 2):
        kept_out[i] = project(attended_ref[...], weight_ref, places_ref[...][2, 0] ^ i)


def finish(places_ref, near_ref, far_ref, residual_ref, bias_ref, out_ref):
    taken = take_rows(places_ref, near_ref, far_ref)
    out_ref[...] = (residual_ref[...].astype(F32) + bias_ref[...].astype(F32) + taken).astype(BF16)


def on_device(devices, parts, query_new, key_new, value_new, residual, dense_weight, dense_bias,
              key_pool, value_pool, page_table, lengths, request_slot, arrival_index):
    rows, width = query_new.shape
    heads = width // HS
    fresh = jnp.concatenate([query_new, key_new, value_new], axis=1)
    near, far, keys = gather_by_doubling(fresh, devices, [0,6<<30,2<<30], functools.partial(turned, key_pool))
    narrow = jax.ShapeDtypeStruct((rows, width), BF16)
    where = places(arrival_index, rows, devices)
    attended, sent, appended_keys, appended_values = pl.pallas_call(
        functools.partial(attend, parts),
        out_shape=(narrow, jax.ShapeDtypeStruct((parts // 2, rows, width), BF16), narrow, narrow),
        in_specs=[VMEM] * 9,
        out_specs=(VMEM, VMEM, ANY, ANY),
        scratch_shapes=[
            pltpu.VMEM((rows, width), BF16),
            pltpu.VMEM((rows, width), BF16),
            pltpu.SemaphoreType.DMA((2,)),
        ],
        compiler_params=pltpu.CompilerParams(vmem_limit_bytes=8 << 20),
    )(where, near, far, rotary_factors(lengths, heads), page_table, lengths[:, None], keys, value_pool, dense_weight)
    kept = pl.pallas_call(
        functools.partial(keep, parts),
        out_shape=jax.ShapeDtypeStruct((parts // 2, rows, width), F32),
        in_specs=[VMEM] * 3,
        out_specs=VMEM,
        cost_estimate=pl.CostEstimate(flops=1 << 30, bytes_accessed=1 << 20, transcendentals=0),
        compiler_params=pltpu.CompilerParams(vmem_limit_bytes=8 << 20),
    )(where, attended, dense_weight)
    near, far = gather_by_doubling(sum_by_halving(kept, sent, parts).astype(BF16), devices, [])
    hidden = pl.pallas_call(
        finish,
        out_shape=narrow,
        in_specs=[VMEM] * 5,
        out_specs=VMEM,
        compiler_params=pltpu.CompilerParams(vmem_limit_bytes=2 << 20),
    )(places(request_slot, rows, devices), near, far, residual, dense_bias[None, :])
    return hidden, appended_keys, appended_values


def solution(mesh):
    rows = P("req", "tp")
    pool = P("req", None, "tp")
    in_specs = (rows,) * 4 + (P("tp", None), P("tp"), pool, pool, P("req", None)) + (P("req"),) * 3
    step = functools.partial(on_device, mesh.shape["req"], mesh.shape["tp"])
    return jax.shard_map(step, mesh=mesh, in_specs=in_specs, out_specs=(rows,) * 3, check_vma=False)
```

```python
import functools

import jax
import jax.numpy as jnp
from jax import lax
from jax.experimental import pallas as pl
from jax.experimental.pallas import tpu as pltpu
from jax.sharding import PartitionSpec as P

HS = 256
CORES = 2
TURN = 4 << 30
BF16 = jnp.bfloat16
F32 = jnp.float32
ANY = pl.BlockSpec(memory_space=pl.ANY)
VMEM = pl.BlockSpec(memory_space=pltpu.VMEM)


def joined(own_ref, other_ref, *rest):
    out_ref = rest[-1]
    count = own_ref.shape[0]
    out_ref[:count] = own_ref[...]
    out_ref[count:] = other_ref[...]


def join(own, other, work, *first):
    return pl.pallas_call(
        joined,
        out_shape=jax.ShapeDtypeStruct((2 * own.shape[0],) + own.shape[1:], own.dtype),
        in_specs=[VMEM, VMEM] + [ANY] * len(first),
        out_specs=VMEM,
        cost_estimate=pl.CostEstimate(flops=work, bytes_accessed=work >> 14, transcendentals=0),
        compiler_params=pltpu.CompilerParams(vmem_limit_bytes=1 << 20),
    )(own, other, *first)


def gather_by_doubling(block, devices, works, beside):
    held = block[None]
    bit = devices // 2
    results = ()
    while True:
        other = lax.ppermute(held, "req", [(i, i ^ bit) for i in range(devices)])
        if bit == 1:
            return (held, other) + results
        extra = beside[bit](held) if bit in beside else ()
        results += extra
        held = join(held, other, works.pop(0) if works else 0, *extra)
        bit //= 2


def places(rows, per, devices):
    apart = (rows // per) ^ lax.axis_index("req").astype(jnp.int32)
    place = jnp.zeros_like(rows)
    bit, weight = devices // 2, 1
    while bit:
        place = place + jnp.where((apart & bit) != 0, weight, 0)
        bit //= 2
        weight *= 2
    return jnp.stack([place, rows % per])


def take_rows(places_ref, near_ref, far_ref):
    count, per, width = near_ref.shape
    rows = lax.broadcasted_iota(jnp.int32, (per, width), 0)
    taken = []
    table = places_ref[...]
    for i in range(table.shape[1]):
        place, row = table[0, i], table[1, i]
        near = near_ref[jnp.minimum(place, count - 1)].astype(F32)
        far = far_ref[jnp.maximum(place - count, 0)].astype(F32)
        block = jnp.where(place < count, near, far)
        taken.append(jnp.sum(jnp.where(rows == row, block, 0.0), axis=0, keepdims=True))
    return jnp.concatenate(taken, axis=0)


def rotary_factors(lengths, heads):
    rotary_dims = HS // 4
    half = rotary_dims // 2
    rates = 10000.0 ** (-2.0 * jnp.arange(half, dtype=F32) / rotary_dims)
    angle = lengths.astype(F32)[:, None] * rates[None, :]
    cosine, sine = jnp.cos(angle), jnp.sin(angle)
    rows = lengths.shape[0]
    none = jnp.zeros((rows, half), F32)
    rest = jnp.zeros((rows, HS - rotary_dims), F32)
    same = jnp.concatenate([cosine, cosine, rest + 1.0], axis=1)
    right = jnp.concatenate([-sine, none, rest], axis=1)
    left = jnp.concatenate([none, sine, rest], axis=1)
    return jnp.stack([jnp.tile(f, (1, heads)) for f in (same, right, left)])


def turn(pages_ref, after_ref, out_ref):
    pages, page, _ = pages_ref.shape
    for p in range(pages):
        out_ref[:, p * page:(p + 1) * page] = pages_ref[p].T


def turned(pool, after):
    pages, page, width = pool.shape
    return pl.pallas_call(
        turn,
        out_shape=jax.ShapeDtypeStruct((width, pages * page), pool.dtype),
        in_specs=[VMEM, ANY],
        out_specs=VMEM,
        cost_estimate=pl.CostEstimate(flops=TURN, bytes_accessed=1 << 20, transcendentals=0),
        compiler_params=pltpu.CompilerParams(vmem_limit_bytes=8 << 20),
    )(pool, after)


def attend(devices, parts, places_ref, near_ref, far_ref, factors_ref, table_ref, lengths_ref,
           keys_ref, values_ref, weight_ref, where_ref, sent_out, keys_out, values_out,
           key_ref, value_ref, sems):
    slots, width = key_ref.shape
    heads = width // HS
    pages, page = values_ref.shape[0], values_ref.shape[1]
    tokens = pages * page
    scale = HS ** (-0.5)

    taken = take_rows(places_ref, near_ref, far_ref)
    query, key, value = (taken[:, i * width:(i + 1) * width] for i in range(3))

    def rotate(x):
        right = pltpu.roll(x, width - HS // 8, 1)
        left = pltpu.roll(x, HS // 8, 1)
        return x * factors_ref[0] + right * factors_ref[1] + left * factors_ref[2]

    query = rotate(query).astype(BF16).astype(F32)
    key = rotate(key).astype(BF16)
    key_ref[...] = key
    value_ref[...] = value.astype(BF16)
    copies = [
        pltpu.make_async_copy(key_ref, keys_out, sems.at[0]),
        pltpu.make_async_copy(value_ref, values_out, sems.at[1]),
    ]
    for copy in copies:
        copy.start()

    lane = lax.broadcasted_iota(jnp.int32, (slots, 128), 1)
    visible = jnp.zeros((slots, 128), jnp.int32)
    for i in range(table_ref.shape[1]):
        left_over = jnp.clip(lengths_ref[...] - i * page, 0, page)
        visible = jnp.where((lane == table_ref[:, i:i + 1]) & (left_over > 0), left_over, visible)

    together = min(2, heads)
    rows, lanes = together * slots, together * HS
    row_head = lax.broadcasted_iota(jnp.int32, (rows, lanes), 0) // slots
    lane_head = lax.broadcasted_iota(jnp.int32, (rows, lanes), 1) // HS
    mine = row_head == lane_head
    place = lax.broadcasted_iota(jnp.int32, (rows, page), 1)
    shown = jnp.concatenate([visible] * together, axis=0)
    shown = [place < shown[:, p:p + 1] for p in range(pages)]
    starts = range(0, width, lanes)

    def score(first):
        spread = [jnp.concatenate([x[:, first:first + lanes]] * together, axis=0) for x in (query, key.astype(F32), value)]
        queries = jnp.where(mine, spread[0], 0.0)
        own_score = jnp.sum(queries * spread[1], axis=1, keepdims=True) * scale
        return jnp.dot(queries.astype(BF16), keys_ref[first:first + lanes], preferred_element_type=F32), own_score, spread[2]

    def soften(scores, own_score, own_value):
        masked = jnp.concatenate(
            [jnp.where(shown[p], scores[:, p * page:(p + 1) * page] * scale, -jnp.inf) for p in range(pages)], axis=1
        )
        top = jnp.maximum(jnp.max(masked, axis=1, keepdims=True), own_score)
        exps = jnp.exp(masked - top)
        own_exp = jnp.exp(own_score - top)
        total = jnp.sum(exps, axis=1, keepdims=True) + own_exp
        return exps.astype(BF16), own_exp * own_value, 1.0 / total

    def gather_values(first, exps, own, share):
        seen = jnp.dot(exps, values_ref[:, :, first:first + lanes].reshape(tokens, lanes), preferred_element_type=F32)
        seen = jnp.where(mine, (seen + own) * share, 0.0)
        return sum(seen[h * slots:(h + 1) * slots] for h in range(together))

    scored = [score(first) for first in starts]
    softened = [soften(*x) for x in scored]
    attended = [gather_values(first, *x) for first, x in zip(starts, softened)]
    attended = jnp.concatenate(attended, axis=1).astype(BF16)

    for part in range(parts):
        columns = weight_ref[:, part * width:(part + 1) * width]
        terms = jnp.dot(attended, columns, preferred_element_type=F32).astype(BF16)
        for device in range(devices):
            first = device % CORES * (width // CORES)
            sent_out[device * parts + part] = terms[:, first:first + width // CORES]
    for copy in copies:
        copy.wait()


def sort(parts, where_ref, terms_ref, mine_out, theirs_out):
    rows, lanes = mine_out.shape
    table = where_ref[...]
    row = lax.broadcasted_iota(jnp.int32, (rows, lanes), 0)
    taken = []
    for i in range(CORES * rows):
        first = table[0, i] * parts
        block = sum(terms_ref[first + part].astype(F32) for part in range(parts))
        taken.append(jnp.sum(jnp.where(row == table[1, i], block, 0.0), axis=0, keepdims=True))
    mine_out[...] = jnp.concatenate(taken[:rows], axis=0).astype(BF16)
    theirs_out[...] = jnp.concatenate(taken[rows:], axis=0).astype(BF16)


def finish(where_ref, mine_ref, other_ref, residual_ref, bias_ref, out_ref):
    first = where_ref[...][2, 0] == 0
    mine, other = mine_ref[...].astype(F32), other_ref[...].astype(F32)
    taken = jnp.concatenate([jnp.where(first, mine, other), jnp.where(first, other, mine)], axis=1)
    out_ref[...] = (residual_ref[...].astype(F32) + bias_ref[...].astype(F32)[None, :] + taken).astype(BF16)


def on_device(devices, parts, query_new, key_new, value_new, residual, dense_weight, dense_bias,
              key_pool, value_pool, page_table, lengths, request_slot, arrival_index):
    rows, width = query_new.shape
    heads = width // HS
    fresh = jnp.concatenate([query_new, key_new, value_new], axis=1)
    other_core = [(i, i ^ 1) for i in range(devices)]

    def integers(after):
        slots, long, _ = lax.optimization_barrier((request_slot, lengths, after))
        return lax.ppermute(slots, "req", other_core), long[:, None]

    def keys_turned(after):
        return (turned(key_pool, after),)

    near, far, slots, column, keys = gather_by_doubling(
        fresh, devices, [0, 3 << 30, 2 << 30], {4: integers, 2: keys_turned}
    )
    narrow = jax.ShapeDtypeStruct((rows, width), BF16)
    half = jax.ShapeDtypeStruct((rows, width // CORES), BF16)
    own_slots, slots, _ = lax.optimization_barrier((request_slot, slots, near))
    slots = jnp.concatenate([own_slots, slots])
    core = lax.axis_index("req").astype(jnp.int32) % CORES
    where = jnp.stack([slots // rows, slots % rows, jnp.full_like(slots, core)])
    sent, appended_keys, appended_values = pl.pallas_call(
        functools.partial(attend, devices, parts),
        out_shape=(jax.ShapeDtypeStruct((devices * parts,) + half.shape, BF16), narrow, narrow),
        in_specs=[VMEM] * 9 + [ANY],
        out_specs=(VMEM, ANY, ANY),
        scratch_shapes=[
            pltpu.VMEM((rows, width), BF16),
            pltpu.VMEM((rows, width), BF16),
            pltpu.SemaphoreType.DMA((2,)),
        ],
        compiler_params=pltpu.CompilerParams(vmem_limit_bytes=8 << 20),
    )(places(arrival_index, rows, devices), near, far, rotary_factors(lengths, heads), page_table, column,
      keys, value_pool, dense_weight, where)
    terms = lax.all_to_all(sent, ("req", "tp"), 0, 0, tiled=True)
    mine, theirs = pl.pallas_call(
        functools.partial(sort, parts),
        out_shape=(half, half),
        in_specs=[VMEM] * 2,
        out_specs=(VMEM, VMEM),
        compiler_params=pltpu.CompilerParams(vmem_limit_bytes=2 << 20),
    )(where, terms)
    hidden = pl.pallas_call(
        finish,
        out_shape=narrow,
        in_specs=[VMEM] * 5,
        out_specs=VMEM,
        compiler_params=pltpu.CompilerParams(vmem_limit_bytes=2 << 20),
    )(where, mine, lax.ppermute(theirs, "req", other_core), residual, dense_bias)
    return hidden, appended_keys, appended_values


def solution(mesh):
    rows = P("req", "tp")
    pool = P("req", None, "tp")
    in_specs = (rows,) * 4 + (P("tp", None), P("tp"), pool, pool, P("req", None)) + (P("req"),) * 3
    step = functools.partial(on_device, mesh.shape["req"], mesh.shape["tp"])
    return jax.shard_map(step, mesh=mesh, in_specs=in_specs, out_specs=(rows,) * 3, check_vma=False)
```

```python
import functools

import jax
import jax.numpy as jnp
from jax import lax
from jax.experimental import pallas as pl
from jax.experimental.pallas import tpu as pltpu
from jax.sharding import PartitionSpec as P

HS = 256
CORES = 2
TURN = 4 << 30
BF16 = jnp.bfloat16
F32 = jnp.float32
ANY = pl.BlockSpec(memory_space=pl.ANY)
VMEM = pl.BlockSpec(memory_space=pltpu.VMEM)


def joined(own_ref, other_ref, *rest):
    out_ref = rest[-1]
    count = own_ref.shape[0]
    out_ref[:count] = own_ref[...]
    out_ref[count:] = other_ref[...]


def join(own, other, work, *first):
    return pl.pallas_call(
        joined,
        out_shape=jax.ShapeDtypeStruct((2 * own.shape[0],) + own.shape[1:], own.dtype),
        in_specs=[VMEM, VMEM] + [ANY] * len(first),
        out_specs=VMEM,
        cost_estimate=pl.CostEstimate(flops=work, bytes_accessed=work >> 14, transcendentals=0),
        compiler_params=pltpu.CompilerParams(vmem_limit_bytes=1 << 20),
    )(own, other, *first)


def gather_by_doubling(block, devices, works, beside):
    held = block[None]
    bit = devices // 2
    results = ()
    while True:
        other = lax.ppermute(held, "req", [(i, i ^ bit) for i in range(devices)])
        if bit == 1:
            return (held, other) + results
        extra = beside[bit](held) if bit in beside else ()
        results += extra
        held = join(held, other, works.pop(0) if works else 0, *extra)
        bit //= 2


def places(rows, per, devices):
    apart = (rows // per) ^ lax.axis_index("req").astype(jnp.int32)
    place = jnp.zeros_like(rows)
    bit, weight = devices // 2, 1
    while bit:
        place = place + jnp.where((apart & bit) != 0, weight, 0)
        bit //= 2
        weight *= 2
    return jnp.stack([place, rows % per])


def take_rows(places_ref, near_ref, far_ref):
    count, per, width = near_ref.shape
    rows = lax.broadcasted_iota(jnp.int32, (per, width), 0)
    taken = []
    table = places_ref[...]
    for i in range(table.shape[1]):
        place, row = table[0, i], table[1, i]
        near = near_ref[jnp.minimum(place, count - 1)].astype(F32)
        far = far_ref[jnp.maximum(place - count, 0)].astype(F32)
        block = jnp.where(place < count, near, far)
        taken.append(jnp.sum(jnp.where(rows == row, block, 0.0), axis=0, keepdims=True))
    return jnp.concatenate(taken, axis=0)


def rotary_factors(lengths, heads):
    rotary_dims = HS // 4
    half = rotary_dims // 2
    rates = 10000.0 ** (-2.0 * jnp.arange(half, dtype=F32) / rotary_dims)
    angle = lengths.astype(F32)[:, None] * rates[None, :]
    cosine, sine = jnp.cos(angle), jnp.sin(angle)
    rows = lengths.shape[0]
    none = jnp.zeros((rows, half), F32)
    rest = jnp.zeros((rows, HS - rotary_dims), F32)
    same = jnp.concatenate([cosine, cosine, rest + 1.0], axis=1)
    right = jnp.concatenate([-sine, none, rest], axis=1)
    left = jnp.concatenate([none, sine, rest], axis=1)
    return jnp.stack([jnp.tile(f, (1, heads)) for f in (same, right, left)])


def turn(pages_ref, after_ref, out_ref):
    pages, page, _ = pages_ref.shape
    for p in range(pages):
        out_ref[:, p * page:(p + 1) * page] = pages_ref[p].T


def turned(pool, after):
    pages, page, width = pool.shape
    return pl.pallas_call(
        turn,
        out_shape=jax.ShapeDtypeStruct((width, pages * page), pool.dtype),
        in_specs=[VMEM, ANY],
        out_specs=VMEM,
        cost_estimate=pl.CostEstimate(flops=TURN, bytes_accessed=1 << 20, transcendentals=0),
        compiler_params=pltpu.CompilerParams(vmem_limit_bytes=8 << 20),
    )(pool, after)


def attend(devices, parts, places_ref, near_ref, far_ref, factors_ref, table_ref, lengths_ref,
           keys_ref, values_ref, weight_ref, where_ref, sent_out, keys_out, values_out,
           key_ref, value_ref, sems):
    slots, width = key_ref.shape
    heads = width // HS
    pages, page = values_ref.shape[0], values_ref.shape[1]
    tokens = pages * page
    scale = HS ** (-0.5)

    taken = take_rows(places_ref, near_ref, far_ref)
    query, key, value = (taken[:, i * width:(i + 1) * width] for i in range(3))

    def rotate(x):
        right = pltpu.roll(x, width - HS // 8, 1)
        left = pltpu.roll(x, HS // 8, 1)
        return x * factors_ref[0] + right * factors_ref[1] + left * factors_ref[2]

    query = rotate(query).astype(BF16).astype(F32)
    key = rotate(key).astype(BF16)
    key_ref[...] = key
    value_ref[...] = value.astype(BF16)
    copies = [
        pltpu.make_async_copy(key_ref, keys_out, sems.at[0]),
        pltpu.make_async_copy(value_ref, values_out, sems.at[1]),
    ]
    for copy in copies:
        copy.start()

    lane = lax.broadcasted_iota(jnp.int32, (slots, 128), 1)
    visible = jnp.zeros((slots, 128), jnp.int32)
    for i in range(table_ref.shape[1]):
        left_over = jnp.clip(lengths_ref[...] - i * page, 0, page)
        visible = jnp.where((lane == table_ref[:, i:i + 1]) & (left_over > 0), left_over, visible)

    together = min(2, heads)
    rows, lanes = together * slots, together * HS
    row_head = lax.broadcasted_iota(jnp.int32, (rows, lanes), 0) // slots
    lane_head = lax.broadcasted_iota(jnp.int32, (rows, lanes), 1) // HS
    mine = row_head == lane_head
    place = lax.broadcasted_iota(jnp.int32, (rows, page), 1)
    shown = jnp.concatenate([visible] * together, axis=0)
    shown = [place < shown[:, p:p + 1] for p in range(pages)]
    starts = range(0, width, lanes)

    def score(first):
        spread = [jnp.concatenate([x[:, first:first + lanes]] * together, axis=0) for x in (query, key.astype(F32), value)]
        queries = jnp.where(mine, spread[0], 0.0)
        own_score = jnp.sum(queries * spread[1], axis=1, keepdims=True) * scale
        return jnp.dot(queries.astype(BF16), keys_ref[first:first + lanes], preferred_element_type=F32), own_score, spread[2]

    def soften(scores, own_score, own_value):
        masked = jnp.concatenate(
            [jnp.where(shown[p], scores[:, p * page:(p + 1) * page] * scale, -jnp.inf) for p in range(pages)], axis=1
        )
        top = jnp.maximum(jnp.max(masked, axis=1, keepdims=True), own_score)
        exps = jnp.exp(masked - top)
        own_exp = jnp.exp(own_score - top)
        total = jnp.sum(exps, axis=1, keepdims=True) + own_exp
        return exps.astype(BF16), own_exp * own_value, 1.0 / total

    def gather_values(first, exps, own, share):
        seen = jnp.dot(exps, values_ref[:, :, first:first + lanes].reshape(tokens, lanes), preferred_element_type=F32)
        seen = jnp.where(mine, (seen + own) * share, 0.0)
        return sum(seen[h * slots:(h + 1) * slots] for h in range(together))

    scored = [score(first) for first in starts]
    softened = [soften(*x) for x in scored]
    attended = [gather_values(first, *x) for first, x in zip(starts, softened)]

    for part in range(parts):
        terms = sum(
            jnp.dot(x.astype(BF16), weight_ref[first:first + lanes, part * width:(part + 1) * width], preferred_element_type=F32)
            for first, x in zip(starts, attended)
        ).astype(BF16)
        for device in range(devices):
            first = device % CORES * (width // CORES)
            sent_out[device * parts + part] = terms[:, first:first + width // CORES]
    for copy in copies:
        copy.wait()


def sort(parts, where_ref, terms_ref, mine_out, theirs_out):
    rows, lanes = mine_out.shape
    table = where_ref[...]
    row = lax.broadcasted_iota(jnp.int32, (rows, lanes), 0)
    taken = []
    for i in range(CORES * rows):
        first = table[0, i] * parts
        block = sum(terms_ref[first + part].astype(F32) for part in range(parts))
        taken.append(jnp.sum(jnp.where(row == table[1, i], block, 0.0), axis=0, keepdims=True))
    mine_out[...] = jnp.concatenate(taken[:rows], axis=0).astype(BF16)
    theirs_out[...] = jnp.concatenate(taken[rows:], axis=0).astype(BF16)


def finish(where_ref, mine_ref, other_ref, residual_ref, bias_ref, out_ref):
    first = where_ref[...][2, 0] == 0
    mine, other = mine_ref[...].astype(F32), other_ref[...].astype(F32)
    taken = jnp.concatenate([jnp.where(first, mine, other), jnp.where(first, other, mine)], axis=1)
    out_ref[...] = (residual_ref[...].astype(F32) + bias_ref[...].astype(F32)[None, :] + taken).astype(BF16)


def on_device(devices, parts, query_new, key_new, value_new, residual, dense_weight, dense_bias,
              key_pool, value_pool, page_table, lengths, request_slot, arrival_index):
    rows, width = query_new.shape
    heads = width // HS
    fresh = jnp.concatenate([query_new, key_new, value_new], axis=1)
    other_core = [(i, i ^ 1) for i in range(devices)]

    def integers(after):
        slots, long, _ = lax.optimization_barrier((request_slot, lengths, after))
        return lax.ppermute(slots, "req", other_core), long[:, None]

    def keys_turned(after):
        return (turned(key_pool, after),)

    near, far, slots, column, keys = gather_by_doubling(
        fresh, devices, [0, 3 << 30, 2 << 30], {4: integers, 2: keys_turned}
    )
    narrow = jax.ShapeDtypeStruct((rows, width), BF16)
    half = jax.ShapeDtypeStruct((rows, width // CORES), BF16)
    own_slots, slots, _ = lax.optimization_barrier((request_slot, slots, near))
    slots = jnp.concatenate([own_slots, slots])
    core = lax.axis_index("req").astype(jnp.int32) % CORES
    where = jnp.stack([slots // rows, slots % rows, jnp.full_like(slots, core)])
    sent, appended_keys, appended_values = pl.pallas_call(
        functools.partial(attend, devices, parts),
        out_shape=(jax.ShapeDtypeStruct((devices * parts,) + half.shape, BF16), narrow, narrow),
        in_specs=[VMEM] * 9 + [ANY],
        out_specs=(VMEM, ANY, ANY),
        scratch_shapes=[
            pltpu.VMEM((rows, width), BF16),
            pltpu.VMEM((rows, width), BF16),
            pltpu.SemaphoreType.DMA((2,)),
        ],
        compiler_params=pltpu.CompilerParams(vmem_limit_bytes=8 << 20),
    )(places(arrival_index, rows, devices), near, far, rotary_factors(lengths, heads), page_table, column,
      keys, value_pool, dense_weight, where)
    terms = lax.all_to_all(sent, ("req", "tp"), 0, 0, tiled=True)
    mine, theirs = pl.pallas_call(
        functools.partial(sort, parts),
        out_shape=(half, half),
        in_specs=[VMEM] * 2,
        out_specs=(VMEM, VMEM),
        compiler_params=pltpu.CompilerParams(vmem_limit_bytes=2 << 20),
    )(where, terms)
    hidden = pl.pallas_call(
        finish,
        out_shape=narrow,
        in_specs=[VMEM] * 5,
        out_specs=VMEM,
        compiler_params=pltpu.CompilerParams(vmem_limit_bytes=2 << 20),
    )(where, mine, lax.ppermute(theirs, "req", other_core), residual, dense_bias)
    return hidden, appended_keys, appended_values


def solution(mesh):
    rows = P("req", "tp")
    pool = P("req", None, "tp")
    in_specs = (rows,) * 4 + (P("tp", None), P("tp"), pool, pool, P("req", None)) + (P("req"),) * 3
    step = functools.partial(on_device, mesh.shape["req"], mesh.shape["tp"])
    return jax.shard_map(step, mesh=mesh, in_specs=in_specs, out_specs=(rows,) * 3, check_vma=False)
```

```python
import functools

import jax
import jax.numpy as jnp
from jax import lax
from jax.experimental import pallas as pl
from jax.experimental.pallas import tpu as pltpu
from jax.sharding import PartitionSpec as P

HS = 256
CORES = 2
TURN = 4 << 30
BF16 = jnp.bfloat16
F32 = jnp.float32
ANY = pl.BlockSpec(memory_space=pl.ANY)
VMEM = pl.BlockSpec(memory_space=pltpu.VMEM)


def joined(own_ref, other_ref, *rest):
    out_ref = rest[-1]
    count = own_ref.shape[0]
    out_ref[:count] = own_ref[...]
    out_ref[count:] = other_ref[...]


def join(own, other, work, *first):
    return pl.pallas_call(
        joined,
        out_shape=jax.ShapeDtypeStruct((2 * own.shape[0],) + own.shape[1:], own.dtype),
        in_specs=[VMEM, VMEM] + [ANY] * len(first),
        out_specs=VMEM,
        cost_estimate=pl.CostEstimate(flops=work, bytes_accessed=work >> 14, transcendentals=0),
        compiler_params=pltpu.CompilerParams(vmem_limit_bytes=1 << 20),
    )(own, other, *first)


def gather_by_doubling(block, devices, works, beside):
    held = block[None]
    bit = devices // 2
    results = ()
    while True:
        other = lax.ppermute(held, "req", [(i, i ^ bit) for i in range(devices)])
        if bit == 1:
            return (held, other) + results
        extra = beside[bit](held) if bit in beside else ()
        results += extra
        held = join(held, other, works.pop(0) if works else 0, *extra)
        bit //= 2


def places(rows, per, devices):
    apart = (rows // per) ^ lax.axis_index("req").astype(jnp.int32)
    place = jnp.zeros_like(rows)
    bit, weight = devices // 2, 1
    while bit:
        place = place + jnp.where((apart & bit) != 0, weight, 0)
        bit //= 2
        weight *= 2
    return jnp.stack([place, rows % per])


def take_rows(places_ref, near_ref, far_ref):
    count, per, width = near_ref.shape
    rows = lax.broadcasted_iota(jnp.int32, (per, width), 0)
    taken = []
    table = places_ref[...]
    for i in range(table.shape[1]):
        place, row = table[0, i], table[1, i]
        near = near_ref[jnp.minimum(place, count - 1)].astype(F32)
        far = far_ref[jnp.maximum(place - count, 0)].astype(F32)
        block = jnp.where(place < count, near, far)
        taken.append(jnp.sum(jnp.where(rows == row, block, 0.0), axis=0, keepdims=True))
    return jnp.concatenate(taken, axis=0)


def rotary_factors(lengths, heads):
    rotary_dims = HS // 4
    half = rotary_dims // 2
    rates = 10000.0 ** (-2.0 * jnp.arange(half, dtype=F32) / rotary_dims)
    angle = lengths.astype(F32)[:, None] * rates[None, :]
    cosine, sine = jnp.cos(angle), jnp.sin(angle)
    rows = lengths.shape[0]
    none = jnp.zeros((rows, half), F32)
    rest = jnp.zeros((rows, HS - rotary_dims), F32)
    same = jnp.concatenate([cosine, cosine, rest + 1.0], axis=1)
    right = jnp.concatenate([-sine, none, rest], axis=1)
    left = jnp.concatenate([none, sine, rest], axis=1)
    return jnp.stack([jnp.tile(f, (1, heads)) for f in (same, right, left)])


def turn(pages_ref, after_ref, out_ref):
    pages, page, _ = pages_ref.shape
    for p in range(pages):
        out_ref[:, p * page:(p + 1) * page] = pages_ref[p].T


def turned(pool, after):
    pages, page, width = pool.shape
    return pl.pallas_call(
        turn,
        out_shape=jax.ShapeDtypeStruct((width, pages * page), pool.dtype),
        in_specs=[VMEM, ANY],
        out_specs=VMEM,
        cost_estimate=pl.CostEstimate(flops=TURN, bytes_accessed=1 << 20, transcendentals=0),
        compiler_params=pltpu.CompilerParams(vmem_limit_bytes=8 << 20),
    )(pool, after)


def attend(devices, parts, places_ref, near_ref, far_ref, factors_ref, table_ref, lengths_ref,
           keys_ref, values_ref, weight_ref, where_ref, sent_out, keys_out, values_out,
           key_ref, value_ref, sems):
    slots, width = key_ref.shape
    heads = width // HS
    pages, page = values_ref.shape[0], values_ref.shape[1]
    tokens = pages * page
    scale = HS ** (-0.5)

    taken = take_rows(places_ref, near_ref, far_ref)
    query, key, value = (taken[:, i * width:(i + 1) * width] for i in range(3))

    def rotate(x):
        right = pltpu.roll(x, width - HS // 8, 1)
        left = pltpu.roll(x, HS // 8, 1)
        return x * factors_ref[0] + right * factors_ref[1] + left * factors_ref[2]

    query = rotate(query).astype(BF16).astype(F32)
    key = rotate(key).astype(BF16)
    key_ref[...] = key
    value_ref[...] = value.astype(BF16)
    copies = [
        pltpu.make_async_copy(key_ref, keys_out, sems.at[0]),
        pltpu.make_async_copy(value_ref, values_out, sems.at[1]),
    ]
    for copy in copies:
        copy.start()

    lane = lax.broadcasted_iota(jnp.int32, (slots, 128), 1)
    visible = jnp.zeros((slots, 128), jnp.int32)
    for i in range(table_ref.shape[1]):
        left_over = jnp.clip(lengths_ref[...] - i * page, 0, page)
        visible = jnp.where((lane == table_ref[:, i:i + 1]) & (left_over > 0), left_over, visible)

    together = min(2, heads)
    rows, lanes = together * slots, together * HS
    row_head = lax.broadcasted_iota(jnp.int32, (rows, lanes), 0) // slots
    lane_head = lax.broadcasted_iota(jnp.int32, (rows, lanes), 1) // HS
    mine = row_head == lane_head
    place = lax.broadcasted_iota(jnp.int32, (rows, page), 1)
    shown = jnp.concatenate([visible] * together, axis=0)
    shown = [place < shown[:, p:p + 1] for p in range(pages)]
    starts = range(0, width, lanes)

    def score(first):
        spread = [jnp.concatenate([x[:, first:first + lanes]] * together, axis=0) for x in (query, key.astype(F32), value)]
        queries = jnp.where(mine, spread[0] * scale, 0.0)
        own_score = jnp.sum(queries * spread[1], axis=1, keepdims=True)
        return jnp.dot(queries.astype(BF16), keys_ref[first:first + lanes], preferred_element_type=F32), own_score, spread[2]

    def soften(scores, own_score, own_value):
        masked = jnp.concatenate(
            [jnp.where(shown[p], scores[:, p * page:(p + 1) * page], -jnp.inf) for p in range(pages)], axis=1
        )
        top = jnp.maximum(jnp.max(masked, axis=1, keepdims=True), own_score)
        exps = jnp.exp(masked - top)
        own_exp = jnp.exp(own_score - top)
        total = jnp.sum(exps, axis=1, keepdims=True) + own_exp
        return exps.astype(BF16), own_exp * own_value, 1.0 / total

    def gather_values(first, exps, own, share):
        seen = jnp.dot(exps, values_ref[:, :, first:first + lanes].reshape(tokens, lanes), preferred_element_type=F32)
        seen = jnp.where(mine, (seen + own) * share, 0.0)
        return sum(seen[h * slots:(h + 1) * slots] for h in range(together))

    scored = [score(first) for first in starts]
    softened = [soften(*x) for x in scored]
    attended = [gather_values(first, *x) for first, x in zip(starts, softened)]

    for part in range(parts):
        terms = sum(
            jnp.dot(x.astype(BF16), weight_ref[first:first + lanes, part * width:(part + 1) * width], preferred_element_type=F32)
            for first, x in zip(starts, attended)
        ).astype(BF16)
        for device in range(devices):
            first = device % CORES * (width // CORES)
            sent_out[device * parts + part] = terms[:, first:first + width // CORES]
    for copy in copies:
        copy.wait()


def sort(parts, where_ref, terms_ref, mine_out, theirs_out):
    rows, lanes = mine_out.shape
    table = where_ref[...]
    row = lax.broadcasted_iota(jnp.int32, (rows, lanes), 0)
    taken = []
    for i in range(CORES * rows):
        first = table[0, i] * parts
        block = sum(terms_ref[first + part].astype(F32) for part in range(parts))
        taken.append(jnp.sum(jnp.where(row == table[1, i], block, 0.0), axis=0, keepdims=True))
    mine_out[...] = jnp.concatenate(taken[:rows], axis=0).astype(BF16)
    theirs_out[...] = jnp.concatenate(taken[rows:], axis=0).astype(BF16)


def finish(where_ref, mine_ref, other_ref, residual_ref, bias_ref, out_ref):
    first = where_ref[...][2, 0] == 0
    mine, other = mine_ref[...].astype(F32), other_ref[...].astype(F32)
    taken = jnp.concatenate([jnp.where(first, mine, other), jnp.where(first, other, mine)], axis=1)
    out_ref[...] = (residual_ref[...].astype(F32) + bias_ref[...].astype(F32)[None, :] + taken).astype(BF16)


def on_device(devices, parts, query_new, key_new, value_new, residual, dense_weight, dense_bias,
              key_pool, value_pool, page_table, lengths, request_slot, arrival_index):
    rows, width = query_new.shape
    heads = width // HS
    fresh = jnp.concatenate([query_new, key_new, value_new], axis=1)
    other_core = [(i, i ^ 1) for i in range(devices)]

    def integers(after):
        slots, long, _ = lax.optimization_barrier((request_slot, lengths, after))
        return lax.ppermute(slots, "req", other_core), long[:, None]

    def keys_turned(after):
        return (turned(key_pool, after),)

    near, far, slots, column, keys = gather_by_doubling(
        fresh, devices, [0, 3 << 30, 2 << 30], {4: integers, 2: keys_turned}
    )
    narrow = jax.ShapeDtypeStruct((rows, width), BF16)
    half = jax.ShapeDtypeStruct((rows, width // CORES), BF16)
    own_slots, slots, _ = lax.optimization_barrier((request_slot, slots, near))
    slots = jnp.concatenate([own_slots, slots])
    core = lax.axis_index("req").astype(jnp.int32) % CORES
    where = jnp.stack([slots // rows, slots % rows, jnp.full_like(slots, core)])
    sent, appended_keys, appended_values = pl.pallas_call(
        functools.partial(attend, devices, parts),
        out_shape=(jax.ShapeDtypeStruct((devices * parts,) + half.shape, BF16), narrow, narrow),
        in_specs=[VMEM] * 9 + [ANY],
        out_specs=(VMEM, ANY, ANY),
        scratch_shapes=[
            pltpu.VMEM((rows, width), BF16),
            pltpu.VMEM((rows, width), BF16),
            pltpu.SemaphoreType.DMA((2,)),
        ],
        compiler_params=pltpu.CompilerParams(vmem_limit_bytes=8 << 20),
    )(places(arrival_index, rows, devices), near, far, rotary_factors(lengths, heads), page_table, column,
      keys, value_pool, dense_weight, where)
    terms = lax.all_to_all(sent, ("req", "tp"), 0, 0, tiled=True)
    mine, theirs = pl.pallas_call(
        functools.partial(sort, parts),
        out_shape=(half, half),
        in_specs=[VMEM] * 2,
        out_specs=(VMEM, VMEM),
        compiler_params=pltpu.CompilerParams(vmem_limit_bytes=2 << 20),
    )(where, terms)
    hidden = pl.pallas_call(
        finish,
        out_shape=narrow,
        in_specs=[VMEM] * 5,
        out_specs=VMEM,
        compiler_params=pltpu.CompilerParams(vmem_limit_bytes=2 << 20),
    )(where, mine, lax.ppermute(theirs, "req", other_core), residual, dense_bias)
    return hidden, appended_keys, appended_values


def solution(mesh):
    rows = P("req", "tp")
    pool = P("req", None, "tp")
    in_specs = (rows,) * 4 + (P("tp", None), P("tp"), pool, pool, P("req", None)) + (P("req"),) * 3
    step = functools.partial(on_device, mesh.shape["req"], mesh.shape["tp"])
    return jax.shard_map(step, mesh=mesh, in_specs=in_specs, out_specs=(rows,) * 3, check_vma=False)
```

```python
import functools

import jax
import jax.numpy as jnp
from jax import lax
from jax.experimental import pallas as pl
from jax.experimental.pallas import tpu as pltpu
from jax.sharding import PartitionSpec as P

HS = 256
CORES = 2
TURN = 4 << 30
BF16 = jnp.bfloat16
F32 = jnp.float32
ANY = pl.BlockSpec(memory_space=pl.ANY)
VMEM = pl.BlockSpec(memory_space=pltpu.VMEM)


def joined(own_ref, other_ref, *rest):
    out_ref = rest[-1]
    count = own_ref.shape[0]
    out_ref[:count] = own_ref[...]
    out_ref[count:] = other_ref[...]


def join(own, other, work, *first):
    return pl.pallas_call(
        joined,
        out_shape=jax.ShapeDtypeStruct((2 * own.shape[0],) + own.shape[1:], own.dtype),
        in_specs=[VMEM, VMEM] + [ANY] * len(first),
        out_specs=VMEM,
        cost_estimate=pl.CostEstimate(flops=work, bytes_accessed=work >> 14, transcendentals=0),
        compiler_params=pltpu.CompilerParams(vmem_limit_bytes=1 << 20),
    )(own, other, *first)


def gather_by_doubling(block, devices, works, beside):
    held = block[None]
    bit = devices // 2
    results = ()
    while True:
        other = lax.ppermute(held, "req", [(i, i ^ bit) for i in range(devices)])
        if bit == 1:
            return (held, other) + results
        extra = beside[bit](held) if bit in beside else ()
        results += extra
        held = join(held, other, works.pop(0) if works else 0, *extra)
        bit //= 2


def places(rows, per, devices):
    apart = (rows // per) ^ lax.axis_index("req").astype(jnp.int32)
    place = jnp.zeros_like(rows)
    bit, weight = devices // 2, 1
    while bit:
        place = place + jnp.where((apart & bit) != 0, weight, 0)
        bit //= 2
        weight *= 2
    return jnp.stack([place, rows % per])


def take_rows(places_ref, near_ref, far_ref):
    count, per, width = near_ref.shape
    rows = lax.broadcasted_iota(jnp.int32, (per, width), 0)
    taken = []
    table = places_ref[...]
    for i in range(table.shape[1]):
        place, row = table[0, i], table[1, i]
        near = near_ref[jnp.minimum(place, count - 1)].astype(F32)
        far = far_ref[jnp.maximum(place - count, 0)].astype(F32)
        block = jnp.where(place < count, near, far)
        taken.append(jnp.sum(jnp.where(rows == row, block, 0.0), axis=0, keepdims=True))
    return jnp.concatenate(taken, axis=0)


def rotary_factors(lengths, heads):
    rotary_dims = HS // 4
    half = rotary_dims // 2
    rates = 10000.0 ** (-2.0 * jnp.arange(half, dtype=F32) / rotary_dims)
    angle = lengths.astype(F32)[:, None] * rates[None, :]
    cosine, sine = jnp.cos(angle), jnp.sin(angle)
    rows = lengths.shape[0]
    none = jnp.zeros((rows, half), F32)
    rest = jnp.zeros((rows, HS - rotary_dims), F32)
    same = jnp.concatenate([cosine, cosine, rest + 1.0], axis=1)
    right = jnp.concatenate([-sine, none, rest], axis=1)
    left = jnp.concatenate([none, sine, rest], axis=1)
    return jnp.stack([jnp.tile(f, (1, heads)) for f in (same, right, left)])


def turn(pages_ref, after_ref, out_ref):
    pages, page, _ = pages_ref.shape
    for p in range(pages):
        out_ref[:, p * page:(p + 1) * page] = pages_ref[p].T


def turned(pool, after):
    pages, page, width = pool.shape
    return pl.pallas_call(
        turn,
        out_shape=jax.ShapeDtypeStruct((width, pages * page), pool.dtype),
        in_specs=[VMEM, ANY],
        out_specs=VMEM,
        cost_estimate=pl.CostEstimate(flops=TURN, bytes_accessed=1 << 20, transcendentals=0),
        compiler_params=pltpu.CompilerParams(vmem_limit_bytes=8 << 20),
    )(pool, after)


def attend(devices, parts, places_ref, near_ref, far_ref, factors_ref, table_ref, lengths_ref,
           keys_ref, values_ref, weight_ref, where_ref, sent_out, keys_out, values_out,
           key_ref, value_ref, sems):
    slots, width = key_ref.shape
    heads = width // HS
    pages, page = values_ref.shape[0], values_ref.shape[1]
    tokens = pages * page
    scale = HS ** (-0.5)

    taken = take_rows(places_ref, near_ref, far_ref)
    query, key, value = (taken[:, i * width:(i + 1) * width] for i in range(3))

    def rotate(x):
        right = pltpu.roll(x, width - HS // 8, 1)
        left = pltpu.roll(x, HS // 8, 1)
        return x * factors_ref[0] + right * factors_ref[1] + left * factors_ref[2]

    query = rotate(query).astype(BF16).astype(F32)
    key = rotate(key).astype(BF16)
    key_ref[...] = key
    value_ref[...] = value.astype(BF16)
    copies = [
        pltpu.make_async_copy(key_ref, keys_out, sems.at[0]),
        pltpu.make_async_copy(value_ref, values_out, sems.at[1]),
    ]
    for copy in copies:
        copy.start()

    lane = lax.broadcasted_iota(jnp.int32, (slots, 128), 1)
    visible = jnp.zeros((slots, 128), jnp.int32)
    for i in range(table_ref.shape[1]):
        left_over = jnp.clip(lengths_ref[...] - i * page, 0, page)
        visible = jnp.where((lane == table_ref[:, i:i + 1]) & (left_over > 0), left_over, visible)

    together = min(2, heads)
    rows, lanes = together * slots, together * HS
    row_head = lax.broadcasted_iota(jnp.int32, (rows, lanes), 0) // slots
    lane_head = lax.broadcasted_iota(jnp.int32, (rows, lanes), 1) // HS
    mine = row_head == lane_head
    place = lax.broadcasted_iota(jnp.int32, (rows, page), 1)
    shown = jnp.concatenate([visible] * together, axis=0)
    shown = [place < shown[:, p:p + 1] for p in range(pages)]
    starts = range(0, width, lanes)

    def score(first):
        spread = [jnp.concatenate([x[:, first:first + lanes]] * together, axis=0) for x in (query, key.astype(F32), value)]
        queries = jnp.where(mine, spread[0] * scale, 0.0)
        own_score = jnp.sum(queries * spread[1], axis=1, keepdims=True)
        return jnp.dot(queries.astype(BF16), keys_ref[first:first + lanes], preferred_element_type=F32), own_score, spread[2]

    def soften(scores, own_score, own_value):
        masked = jnp.concatenate(
            [jnp.where(shown[p], scores[:, p * page:(p + 1) * page], -jnp.inf) for p in range(pages)], axis=1
        )
        top = jnp.maximum(jnp.max(masked, axis=1, keepdims=True), own_score)
        exps = jnp.exp(masked - top)
        own_exp = jnp.exp(own_score - top)
        total = jnp.sum(exps, axis=1, keepdims=True) + own_exp
        return exps.astype(BF16), own_exp * own_value, 1.0 / total

    def gather_values(first, exps, own, share):
        seen = sum(
            jnp.dot(
                exps[:, p * page:(p + pages // 2) * page],
                values_ref[p:p + pages // 2, :, first:first + lanes].reshape(tokens // 2, lanes),
                preferred_element_type=F32,
            )
            for p in (0, pages // 2)
        )
        seen = jnp.where(mine, (seen + own) * share, 0.0)
        return sum(seen[h * slots:(h + 1) * slots] for h in range(together))

    scored = [score(first) for first in starts]
    softened = [soften(*x) for x in scored]
    attended = [gather_values(first, *x) for first, x in zip(starts, softened)]

    for part in range(parts):
        terms = sum(
            jnp.dot(x.astype(BF16), weight_ref[first:first + lanes, part * width:(part + 1) * width], preferred_element_type=F32)
            for first, x in zip(starts, attended)
        ).astype(BF16)
        for device in range(devices):
            first = device % CORES * (width // CORES)
            sent_out[device * parts + part] = terms[:, first:first + width // CORES]
    for copy in copies:
        copy.wait()


def sort(parts, where_ref, terms_ref, mine_out, theirs_out):
    rows, lanes = mine_out.shape
    table = where_ref[...]
    row = lax.broadcasted_iota(jnp.int32, (rows, lanes), 0)
    taken = []
    for i in range(CORES * rows):
        first = table[0, i] * parts
        block = sum(terms_ref[first + part].astype(F32) for part in range(parts))
        taken.append(jnp.sum(jnp.where(row == table[1, i], block, 0.0), axis=0, keepdims=True))
    mine_out[...] = jnp.concatenate(taken[:rows], axis=0).astype(BF16)
    theirs_out[...] = jnp.concatenate(taken[rows:], axis=0).astype(BF16)


def finish(where_ref, mine_ref, other_ref, residual_ref, bias_ref, out_ref):
    first = where_ref[...][2, 0] == 0
    mine, other = mine_ref[...].astype(F32), other_ref[...].astype(F32)
    taken = jnp.concatenate([jnp.where(first, mine, other), jnp.where(first, other, mine)], axis=1)
    out_ref[...] = (residual_ref[...].astype(F32) + bias_ref[...].astype(F32)[None, :] + taken).astype(BF16)


def on_device(devices, parts, query_new, key_new, value_new, residual, dense_weight, dense_bias,
              key_pool, value_pool, page_table, lengths, request_slot, arrival_index):
    rows, width = query_new.shape
    heads = width // HS
    fresh = jnp.concatenate([query_new, key_new, value_new], axis=1)
    other_core = [(i, i ^ 1) for i in range(devices)]

    def integers(after):
        slots, long, _ = lax.optimization_barrier((request_slot, lengths, after))
        return lax.ppermute(slots, "req", other_core), long[:, None]

    def keys_turned(after):
        return (turned(key_pool, after),)

    near, far, slots, column, keys = gather_by_doubling(
        fresh, devices, [0, 3 << 30, 2 << 30], {4: integers, 2: keys_turned}
    )
    narrow = jax.ShapeDtypeStruct((rows, width), BF16)
    half = jax.ShapeDtypeStruct((rows, width // CORES), BF16)
    own_slots, slots, _ = lax.optimization_barrier((request_slot, slots, near))
    slots = jnp.concatenate([own_slots, slots])
    core = lax.axis_index("req").astype(jnp.int32) % CORES
    where = jnp.stack([slots // rows, slots % rows, jnp.full_like(slots, core)])
    sent, appended_keys, appended_values = pl.pallas_call(
        functools.partial(attend, devices, parts),
        out_shape=(jax.ShapeDtypeStruct((devices * parts,) + half.shape, BF16), narrow, narrow),
        in_specs=[VMEM] * 9 + [ANY],
        out_specs=(VMEM, ANY, ANY),
        scratch_shapes=[
            pltpu.VMEM((rows, width), BF16),
            pltpu.VMEM((rows, width), BF16),
            pltpu.SemaphoreType.DMA((2,)),
        ],
        compiler_params=pltpu.CompilerParams(vmem_limit_bytes=8 << 20),
    )(places(arrival_index, rows, devices), near, far, rotary_factors(lengths, heads), page_table, column,
      keys, value_pool, dense_weight, where)
    terms = lax.all_to_all(sent, ("req", "tp"), 0, 0, tiled=True)
    mine, theirs = pl.pallas_call(
        functools.partial(sort, parts),
        out_shape=(half, half),
        in_specs=[VMEM] * 2,
        out_specs=(VMEM, VMEM),
        compiler_params=pltpu.CompilerParams(vmem_limit_bytes=2 << 20),
    )(where, terms)
    hidden = pl.pallas_call(
        finish,
        out_shape=narrow,
        in_specs=[VMEM] * 5,
        out_specs=VMEM,
        compiler_params=pltpu.CompilerParams(vmem_limit_bytes=2 << 20),
    )(where, mine, lax.ppermute(theirs, "req", other_core), residual, dense_bias)
    return hidden, appended_keys, appended_values


def solution(mesh):
    rows = P("req", "tp")
    pool = P("req", None, "tp")
    in_specs = (rows,) * 4 + (P("tp", None), P("tp"), pool, pool, P("req", None)) + (P("req"),) * 3
    step = functools.partial(on_device, mesh.shape["req"], mesh.shape["tp"])
    return jax.shard_map(step, mesh=mesh, in_specs=in_specs, out_specs=(rows,) * 3, check_vma=False)
```
